32 devices in a mesh: seq: 8 (over z, y), head: 4 (over x, core).
Axes of the slice: x: 2, y: 2, z: 4, core: 2. Of those that a mesh axis runs over, the one named last changes fastest.
Arguments:
- queries: bfloat16 [1024, 2048], P('seq', 'head'), may hold values from -6 to 6
- vision: bfloat16 [1600, 8192], P('seq'), may hold values from -6 to 6
- kv_weight: bfloat16 [2, 8192, 256], P(None, None, 'head'), may hold values from -0.75 to 0.75
- out_weight: bfloat16 [2048, 8192], P('head', 'seq'), may hold values from -0.1875 to 0.1875
- q_gain: float32 [128], replicated, may hold values from 0.1 to 1.9
- k_gain: float32 [128], replicated, may hold values from 0.1 to 1.9
- tile_counts: int32 [4], replicated, may hold values from 200 to 400, as said below
- spans: int32 [1024, 2], P('seq'), may hold values from 0 to 4, as said below
Outputs:
- output: bfloat16 [1024, 8192], P('seq', 'head')
The draws below stay inside these ranges and needn't reach their ends.
Inputs may be any that keep to these rules, and one draw needn't show every extreme that they name: `tile_counts`: every tile holds at least 200 vision tokens in its first slots; one tile is full with exactly 400. For every token spans[t, 0] < spans[t, 1], so each token attends one or more whole tiles.
All inputs are finite; a program needn't handle non-finite values.
Results may differ from the reference program's by a relative error of at most 0.0085.
Values may be sent and summed in bfloat16 or wider, within the bound.
A program may use at most 64 MiB of HBM per device.

```python
import math
import jax
import jax.numpy as jnp
from jax import lax

D = 8192
HD = 128
GROUP = 8
TILES = 4
QH = 16
KV_HEADS = 2
TEXT = 1024
VIS = 1600
CAP = 400


def draw_tile_counts(key, part):
    counts = jax.random.randint(jax.random.fold_in(key, 11), (TILES,), CAP // 2, CAP + 1)
    chosen_tile = jax.random.randint(jax.random.fold_in(key, 12), (), 0, TILES)
    return jnp.where(jnp.arange(TILES) == chosen_tile, CAP, counts).astype(jnp.int32)


def draw_spans(key, part):
    first_tile = jax.random.randint(jax.random.fold_in(key, 21), (TEXT,), 0, TILES)
    tile_span = jax.random.randint(jax.random.fold_in(key, 22), (TEXT,), 1, TILES + 1)
    end_tile = jnp.minimum(first_tile + tile_span, TILES)
    lead_row = jnp.arange(TEXT) == 0
    first_tile = jnp.where(lead_row, 0, first_tile)
    end_tile = jnp.where(lead_row, TILES, end_tile)
    return jnp.stack([first_tile, end_tile], axis=1).astype(jnp.int32)


def with_spikes(entries, rng, source, target, blocks, factor):
    owner, partner = [(jnp.arange(entries.shape[position]) // (entries.shape[position] // blocks)).reshape([-1 if axis == position else 1 for axis in range(entries.ndim)]) for position in (source, target)]
    chosen = jax.random.permutation(rng, blocks)[partner]
    strong = (owner == chosen) | (owner == (partner + blocks // 2) % blocks)
    return jnp.where(strong, factor * entries, entries)


def block_levels(stream_key, dims, split, smallest, high):
    def one(position, blocks):
        steps = jax.random.uniform(jax.random.fold_in(jax.random.fold_in(stream_key, 6), position), (blocks,), jnp.float32, smallest / len(split), high / len(split))
        return jnp.repeat(jnp.exp(steps), dims[position] // blocks).reshape((-1,) + (1,) * (len(dims) - position - 1))

    loudness = one(*split[0])
    for cut in split[1:]:
        loudness = loudness * one(*cut)
    return loudness


def bell_draw(key, dims, width, most, shards=(), kind=jnp.bfloat16):
    result = width * jax.random.normal(key, dims, jnp.float32)
    if shards:
        result = result * block_levels(key, dims, shards, -0.22, 0.18)
    return jnp.clip(result, -most, most).astype(kind)


def heavy_noise(stream_key, dims, deviation, reach, cuts, heavy, held_as=jnp.bfloat16):
    array = deviation * jax.random.normal(stream_key, dims, jnp.float32)
    if cuts:
        array = array * block_levels(stream_key, dims, cuts, -0.22, 0.18)
    return jnp.clip(with_spikes(array, jax.random.fold_in(stream_key, 3), *heavy), -reach, reach).astype(held_as)


def setup_inputs(seed: int = 0) -> dict:
    streams_of = jax.random.split(jax.random.key(seed), 9)
    return {
        "queries": bell_draw(streams_of[0], (TEXT, QH * HD), 1.0, 6.0, ((0, 8), (1, 4))),
        "vision": bell_draw(streams_of[1], (VIS, D), 1.0, 6.0, ((0, 8),)),
        "kv_weight": bell_draw(streams_of[2], (2, D, KV_HEADS * HD), (HD // 2) ** -0.5, 0.75, ((2, 4),)),
        "out_weight": heavy_noise(streams_of[3], (QH * HD, D), (QH * HD) ** -0.5, 0.1875, ((0, 4), (1, 8)), (0, 1, 8, 2.0)),
        "q_gain": jnp.clip(1.0 + 0.18 * jax.random.normal(streams_of[4], (HD,), jnp.float32), 0.1, 1.9),
        "k_gain": jnp.clip(1.0 + 0.18 * jax.random.normal(streams_of[5], (HD,), jnp.float32), 0.1, 1.9),
        "tile_counts": draw_tile_counts(jax.random.fold_in(streams_of[8], 71), 0),
        "spans": draw_spans(jax.random.fold_in(streams_of[8], 71), 0),
    }


EPSILON = 1e-05

def rms_scale(field, gain):
    mean_sq = lax.optimization_barrier(jnp.mean(field * field, axis=-1, keepdims=True))
    return field / jnp.sqrt(mean_sq + EPSILON) * gain

def reference(queries, vision, kv_weight, out_weight, q_gain, k_gain, tile_counts, spans):
    query_f = queries.astype(jnp.float32).reshape(TEXT, QH, HD)
    q_normed = rms_scale(query_f, q_gain).astype(jnp.bfloat16)
    key_raw = jnp.dot(vision, kv_weight[0], preferred_element_type=jnp.float32).reshape(VIS, KV_HEADS, HD)
    keys = rms_scale(key_raw, k_gain).astype(jnp.bfloat16)
    values = jnp.dot(vision, kv_weight[1], preferred_element_type=jnp.float32).astype(jnp.bfloat16).reshape(VIS, KV_HEADS, HD)
    key_index = jnp.arange(VIS, dtype=jnp.int32)
    tile_of = key_index // CAP
    slot_of = key_index % CAP
    present = slot_of < tile_counts[tile_of]
    allowed = present[None, :] & (spans[:, 0:1] <= tile_of[None, :]) & (tile_of[None, :] < spans[:, 1:2])
    q_heads = jnp.transpose(q_normed, (1, 0, 2))
    k_heads = jnp.transpose(keys, (1, 0, 2))
    v_heads = jnp.transpose(values, (1, 0, 2))
    factor = 1.0 / math.sqrt(HD)

    def one_head(head_index):
        group_index = head_index // GROUP
        scores = jnp.dot(q_heads[head_index], k_heads[group_index].T, preferred_element_type=jnp.float32) * factor
        weights = jnp.where(allowed, jnp.exp(scores), jnp.zeros_like(scores))
        totals = lax.optimization_barrier(jnp.sum(weights, axis=1))
        numer = jnp.dot(weights.astype(jnp.bfloat16), v_heads[group_index], preferred_element_type=jnp.float32)
        return (numer / totals[:, None]).astype(jnp.bfloat16)
    attended = lax.map(one_head, jnp.arange(QH, dtype=jnp.int32))
    attended = jnp.transpose(attended, (1, 0, 2)).reshape(TEXT, QH * HD)
    return jnp.dot(attended, out_weight, preferred_element_type=jnp.float32).astype(jnp.bfloat16)
```

```python
import functools
import math

import jax
import jax.numpy as jnp
from jax import lax
from jax.experimental import pallas as pl
from jax.experimental.pallas import tpu as pltpu
from jax.sharding import PartitionSpec as P

HD = 128
TILES = 4
EPSILON = 1e-05
MESH = pl.DeviceIdType.MESH
NT = (((1,), (1,)), ((), ()))
NN = (((1,), (0,)), ((), ()))
CHUNK = 1024


def dot(x, y, dims=NN):
    return lax.dot_general(x, y, dims, preferred_element_type=jnp.float32)


def kernel(
    ns, nh, q_ref, x_ref, w_ref, ow_ref, qg_ref, kg_ref, cnt_ref, span_ref, out_ref,
    acc, sq_own, sq_other, kv, att, keep, send0, recv0, sends, recvs, fin, pieces,
    sq_ss, sq_rs, kv_ss, kv_rs, a_ss, a_rs, l_ss, l_rs, f_ss, f_rs,
):
    seq = lax.axis_index("seq")
    head = lax.axis_index("head")
    ratio = ns // nh
    levels = int(math.log2(nh))
    chain = ns // 2
    place, side = seq // 2, seq % 2
    core = head % 2
    rows = q_ref.shape[0]
    heads_here = q_ref.shape[1] // HD
    vis = x_ref.shape[0]
    pad = kv.shape[2]
    half = ow_ref.shape[1] // 2
    mate = head + 1 - 2 * core
    across = seq + 1 - 2 * side
    has_left, has_right = place > 0, place < chain - 1

    def bit(level):
        return (head // 2**level) % 2

    def partner(level):
        return head + 2**level * (1 - 2 * bit(level))

    barrier = pltpu.get_barrier_semaphore()

    def greet(s, h):
        pl.semaphore_signal(barrier, inc=1, device_id=(s, h), device_id_type=MESH)

    @pl.when(has_left)
    def _():
        greet(seq - 2, head)

    @pl.when(has_right)
    def _():
        greet(seq + 2, head)

    greet(across, head)
    for level in range(levels):
        greet(seq, partner(level))
    for j in range(ratio):
        for h in range(nh):
            source = ratio * head + j

            @pl.when(jnp.logical_or(source != seq, head != h))
            def _():
                greet(source, h)

    acc[...] = jnp.zeros_like(acc)

    def project(i, carry):
        at = pl.ds(pl.multiple_of(i * CHUNK, CHUNK), CHUNK)
        acc[0:vis, :] += dot(x_ref[:, at], w_ref[:, at], NT)
        return carry

    lax.fori_loop(0, x_ref.shape[1] // CHUNK, project, 0)
    raw = acc[...]
    lane = lax.broadcasted_iota(jnp.int32, (1, HD), 1)
    low = lane < HD // 2
    squares = jnp.sum(jnp.where(low, raw * raw, 0.0), axis=1, keepdims=True)
    sq_own[...] = jnp.broadcast_to(squares, sq_own.shape)

    expected = (
        jnp.where(has_left, 1, 0) + jnp.where(has_right, 1, 0) + 1 + levels + ns
        - jnp.where(seq // ratio == head, 1, 0)
    )
    pl.semaphore_wait(barrier, expected)

    sq_copy = pltpu.make_async_remote_copy(
        src_ref=sq_own, dst_ref=sq_other, send_sem=sq_ss, recv_sem=sq_rs,
        device_id=(seq, mate), device_id_type=MESH,
    )
    sq_copy.start()
    left_half, right_half = [], []
    for h in range(heads_here):
        field = q_ref[:, h * HD : (h + 1) * HD].astype(jnp.float32)
        mean_sq = jnp.mean(field * field, axis=1, keepdims=True)
        normed = field / jnp.sqrt(mean_sq + EPSILON) * qg_ref[...]
        swapped = pltpu.roll(normed, HD // 2, 1)
        left_half.append(jnp.where(low, 0.0, swapped).astype(jnp.bfloat16))
        right_half.append(jnp.where(low, swapped, 0.0).astype(jnp.bfloat16))
    sq_copy.wait()
    inverse = 1.0 / jnp.sqrt((sq_own[...] + sq_other[...]) / HD + EPSILON)
    gain = kg_ref[...]
    gain = jnp.where(core == 0, gain, pltpu.roll(gain, HD // 2, 1))
    block = jnp.where(low, raw * inverse * gain, raw)
    block = jnp.where(core == 0, pltpu.roll(block, HD // 2, 1), block)
    kv[core, seq] = block.astype(jnp.bfloat16)

    def nearest(i):
        both = jnp.minimum(place, chain - 1 - place)
        t = (i + 1) // 2
        near = jnp.where(i % 2 == 1, place - t, place + t)
        far = jnp.where(has_right & (place < chain - 1 - place), place + (i - both), place - (i - both))
        return jnp.where(i <= 2 * both, near, far)

    def kv_copy(s, kind, target):
        return pltpu.make_async_remote_copy(
            src_ref=kv.at[core, s], dst_ref=kv.at[core, s],
            send_sem=kv_ss.at[s, kind], recv_sem=kv_rs.at[core, s],
            device_id=target, device_id_type=MESH,
        )

    def a_copy(s, kind, target):
        return pltpu.make_async_remote_copy(
            src_ref=att.at[s], dst_ref=att.at[s],
            send_sem=a_ss.at[s, kind], recv_sem=a_rs.at[s],
            device_id=target, device_id_type=MESH,
        )

    def onward(copy, at, s, act):
        @pl.when(jnp.logical_and(at <= place, has_right))
        def _():
            act(copy(s, 0, (seq + 2, head)))

        @pl.when(jnp.logical_and(at >= place, has_left))
        def _():
            act(copy(s, 1, (seq - 2, head)))

        act(copy(s, 2, (across, head)))

    def start(copy):
        copy.start()

    def wait_send(copy):
        copy.wait_send()

    def kv_step(i, carry):
        @pl.when(i < chain)
        def _():
            at = nearest(i)
            s = 2 * at + side

            @pl.when(i > 0)
            def _():
                kv_copy(s, 3, (seq, mate)).wait_recv()

            onward(kv_copy, at, s, start)
            kv_copy(s, 3, (seq, mate)).start()

        @pl.when(i > 0)
        def _():
            s = 2 * nearest(i - 1) + 1 - side
            kv_copy(s, 3, (seq, mate)).wait_recv()
            kv_copy(s, 3, (seq, mate)).start()

        return carry

    lax.fori_loop(0, chain + 1, kv_step, 0)

    def kv_from_mate(s, carry):
        pltpu.make_async_remote_copy(
            src_ref=kv.at[1 - core, s], dst_ref=kv.at[1 - core, s],
            send_sem=kv_ss.at[s, 3], recv_sem=kv_rs.at[1 - core, s],
            device_id=(seq, mate), device_id_type=MESH,
        ).wait_recv()
        return carry

    lax.fori_loop(0, ns, kv_from_mate, 0)

    slots = ns * pad
    cap = ns * vis // TILES
    j = lax.broadcasted_iota(jnp.int32, (1, slots), 1)
    owner = ((j.astype(jnp.float32) + 0.5) * (1.0 / pad)).astype(jnp.int32)
    inside = j - owner * pad
    token = owner * vis + inside
    tile = jnp.zeros_like(token)
    count = jnp.full_like(token, cnt_ref[0])
    for t in range(1, TILES):
        tile = jnp.where(token >= t * cap, t, tile)
        count = jnp.where(token >= t * cap, t * cap + cnt_ref[t], count)
    present = jnp.logical_and(inside < vis, token < count)
    tile = jnp.where(present, tile, 2 * TILES).astype(jnp.float32)
    span_f = span_ref[...].astype(jnp.float32)
    first = jnp.transpose(jnp.broadcast_to(span_f[0:1, :], (HD, rows)))[:, 0:1]
    end = jnp.transpose(jnp.broadcast_to(span_f[1:2, :], (HD, rows)))[:, 0:1]
    allowed = jnp.logical_and(first <= tile, tile < end)
    scale = math.log2(math.e) / math.sqrt(HD)
    both = jnp.concatenate(
        [kv[0].reshape(slots, HD), kv[1].reshape(slots, HD)], axis=1
    )
    for h in range(heads_here):
        query = jnp.concatenate([left_half[h], right_half[h]], axis=1)
        weights = jnp.where(allowed, jnp.exp2(dot(query, both, NT) * scale), 0.0)
        total = jnp.sum(weights, axis=1, keepdims=True)
        numer = dot(weights.astype(jnp.bfloat16), both)
        numer = jnp.where(low, numer[:, :HD], numer[:, HD:])
        att[seq, :, h * HD : (h + 1) * HD] = (numer / total).astype(jnp.bfloat16)

    def level_refs(level):
        if level == 0:
            return send0, recv0
        return sends[level - 1], recvs[level - 1]

    def level_copy(level, s):
        source, target = level_refs(level)
        return pltpu.make_async_remote_copy(
            src_ref=source.at[s], dst_ref=target.at[s],
            send_sem=l_ss.at[level, s], recv_sem=l_rs.at[level, s],
            device_id=(seq, partner(level)), device_id_type=MESH,
        )

    def final_copy(s):
        return pltpu.make_async_remote_copy(
            src_ref=fin.at[s], dst_ref=pieces.at[seq % ratio, head],
            send_sem=f_ss.at[s], recv_sem=f_rs.at[seq % ratio, head],
            device_id=(s, seq // ratio), device_id_type=MESH,
        )

    def is_mine(s):
        return jnp.logical_and(s == seq, seq // ratio == head)

    def turn(i):
        chained = jnp.where(i == 0, 0, (i + 1) // 2)
        swapped = jnp.where(i == ns - 1, chain - 1, jnp.maximum(i // 2 - 1, 0))
        own_side = jnp.logical_or(i == 0, jnp.logical_and(i % 2 == 1, i < ns - 1))
        at = nearest(jnp.where(own_side, chained, swapped))
        return at, 2 * at + jnp.where(own_side, side, 1 - side), own_side

    sizes = [rows] + [rows >> level for level in range(1, levels)]

    def kept_at(level):
        off = 0
        for done in range(1, level + 1):
            off = off + bit(done) * sizes[done]
        return off

    def first_stage(i):
        at, s, own_side = turn(i)

        @pl.when(i > 0)
        def _():
            a_copy(s, 2, (across, head)).wait_recv()

        @pl.when(own_side)
        def _():
            onward(a_copy, at, s, start)

        rows_in = att[s]
        other = pl.ds(pl.multiple_of((1 - core) * half, half), half)
        send0[s] = dot(rows_in, ow_ref[:, other]).astype(jnp.bfloat16)
        level_copy(0, s).start()
        mine = pl.ds(pl.multiple_of(core * half, half), half)
        keep[s] = dot(rows_in, ow_ref[:, mine])

    def later_stage(level, i):
        _, s, _ = turn(i)
        level_copy(level - 1, s).wait_recv()
        size = sizes[level - 1]
        base = kept_at(level - 1)
        arrived = level_refs(level - 1)[1]
        if level == levels:
            total = keep[s, pl.ds(pl.multiple_of(base, size), size)] + arrived[s].astype(jnp.float32)
            fin[s] = total.astype(jnp.bfloat16)

            @pl.when(is_mine(s))
            def _():
                pieces[seq % ratio, head] = fin[s]

            @pl.when(jnp.logical_not(is_mine(s)))
            def _():
                final_copy(s).start()

        else:
            step = sizes[level]
            out_off = (1 - bit(level)) * step
            in_off = bit(level) * step
            sent = keep[s, pl.ds(pl.multiple_of(base + out_off, step), step)]
            sent = sent + arrived[s, pl.ds(pl.multiple_of(out_off, step), step)].astype(jnp.float32)
            level_refs(level)[0][s] = sent.astype(jnp.bfloat16)
            level_copy(level, s).start()
            at = pl.ds(pl.multiple_of(base + in_off, step), step)
            keep[s, at] = keep[s, at] + arrived[s, pl.ds(pl.multiple_of(in_off, step), step)].astype(jnp.float32)

    def pipeline(i, carry):
        for level in range(levels, 0, -1):
            @pl.when(jnp.logical_and(i >= level, i - level < ns))
            def _():
                later_stage(level, i - level)

        @pl.when(i < ns)
        def _():
            first_stage(i)

        return carry

    lax.fori_loop(0, ns + levels, pipeline, 0)

    for b in range(ratio):
        for h in range(nh):
            @pl.when(jnp.logical_or(ratio * head + b != seq, head != h))
            def _():
                pltpu.make_async_remote_copy(
                    src_ref=fin.at[0], dst_ref=pieces.at[b, h],
                    send_sem=f_ss.at[0], recv_sem=f_rs.at[b, h],
                    device_id=(across, head), device_id_type=MESH,
                ).wait_recv()

            off = sum(((h >> level) & 1) * sizes[level] for level in range(1, levels))
            col = b * 2 * half + (h & 1) * half
            out_ref[off : off + sizes[-1], col : col + half] = pieces[b, h]

    def finish(s, carry):
        at = s // 2

        @pl.when(s % 2 == side)
        def _():
            onward(kv_copy, at, s, wait_send)
            onward(a_copy, at, s, wait_send)

        kv_copy(s, 3, (seq, mate)).wait_send()
        for level in range(levels):
            level_copy(level, s).wait_send()

        @pl.when(jnp.logical_not(is_mine(s)))
        def _():
            final_copy(s).wait_send()

        return carry

    lax.fori_loop(0, ns, finish, 0)


def local(queries, vision, kv_weight, out_weight, q_gain, k_gain, tile_counts, spans):
    ns, nh = lax.axis_size("seq"), lax.axis_size("head")
    rows, width = queries.shape
    vis, model = vision.shape
    cols = out_weight.shape[1]
    half = cols // 2
    levels = int(math.log2(nh))
    pad = -(-vis // 16) * 16
    weights = jnp.swapaxes(kv_weight, 1, 2).reshape(-1, model)
    bf16, f32 = jnp.bfloat16, jnp.float32
    halved = [pltpu.VMEM((ns, rows >> level, half), bf16) for level in range(1, levels)]
    last = rows >> (levels - 1)
    vmem = pl.BlockSpec(memory_space=pltpu.VMEM)
    dma = pltpu.SemaphoreType.DMA
    return pl.pallas_call(
        functools.partial(kernel, ns, nh),
        out_shape=jax.ShapeDtypeStruct((rows, model // nh), bf16),
        in_specs=[vmem] * 6 + [pl.BlockSpec(memory_space=pltpu.SMEM), vmem],
        out_specs=vmem,
        scratch_shapes=[
            pltpu.VMEM((pad, HD), f32),
            pltpu.VMEM((pad, HD), f32),
            pltpu.VMEM((pad, HD), f32),
            pltpu.VMEM((2, ns, pad, HD), bf16),
            pltpu.VMEM((ns, rows, width), bf16),
            pltpu.VMEM((ns, rows, half), f32),
            pltpu.VMEM((ns, rows, half), bf16),
            pltpu.VMEM((ns, rows, half), bf16),
            halved,
            list(halved),
            pltpu.VMEM((ns, last, half), bf16),
            pltpu.VMEM((ns // nh, nh, last, half), bf16),
            dma, dma, dma((ns, 4)), dma((2, ns)), dma((ns, 3)), dma((ns,)),
            dma((levels, ns)), dma((levels, ns)), dma((ns,)), dma((ns // nh, nh)),
        ],
        compiler_params=pltpu.CompilerParams(
            collective_id=0, has_side_effects=True, vmem_limit_bytes=48 * 2**20
        ),
    )(
        queries, vision, weights, out_weight, q_gain.reshape(1, HD), k_gain.reshape(1, HD),
        tile_counts, jnp.swapaxes(spans, 0, 1),
    )


def solution(mesh):
    return jax.shard_map(
        local,
        mesh=mesh,
        in_specs=(
            P("seq", "head"),
            P("seq", None),
            P(None, None, "head"),
            P("head", "seq"),
            P(),
            P(),
            P(),
            P("seq", None),
        ),
        out_specs=P("seq", "head"),
        check_vma=False,
    )
```

```python
import functools
import math

import jax
import jax.numpy as jnp
from jax import lax
from jax.experimental import pallas as pl
from jax.experimental.pallas import tpu as pltpu
from jax.sharding import PartitionSpec as P

HD = 128
TILES = 4
EPSILON = 1e-05
MESH = pl.DeviceIdType.MESH
NT = (((1,), (1,)), ((), ()))
NN = (((1,), (0,)), ((), ()))
CHUNK = 1024


def dot(x, y, dims=NN):
    return lax.dot_general(x, y, dims, preferred_element_type=jnp.float32)


def kernel(
    ns, nh, q_hbm, x_hbm, w_hbm, ow_hbm, qg_hbm, kg_hbm, cnt_hbm, span_hbm, out_ref,
    q_ref, x_ref, w_ref, ow_ref, qg_ref, kg_ref, cnt_ref, span_ref, in_sem, x_sem, w_sem,
    numer, wsum, acc, sq_own, sq_other, kv, att, keep, send0, recv0, sends, recvs, fin, pieces,
    sq_ss, sq_rs, kv_ss, kv_rs, a_ss, a_rs, l_ss, l_rs, f_ss, f_rs,
):
    seq = lax.axis_index("seq")
    head = lax.axis_index("head")
    ratio = ns // nh
    levels = int(math.log2(nh))
    chain = ns // 2
    place, side = seq // 2, seq % 2
    core = head % 2
    rows = q_ref.shape[0]
    heads_here = q_ref.shape[1] // HD
    vis = x_ref.shape[0]
    pad = kv.shape[2]
    half = ow_ref.shape[1] // 2
    mate = head + 1 - 2 * core
    across = seq + 1 - 2 * side

    def bit(level):
        return (head // 2**level) % 2

    def partner(level):
        return head + 2**level * (1 - 2 * bit(level))

    chunks = x_ref.shape[1] // CHUNK

    def x_copy(i):
        at = pl.ds(pl.multiple_of(i * CHUNK, CHUNK), CHUNK)
        return pltpu.make_async_copy(x_hbm.at[:, at], x_ref.at[:, at], x_sem.at[i])

    def w_copy(i):
        at = pl.ds(pl.multiple_of(i * CHUNK, CHUNK), CHUNK)
        return pltpu.make_async_copy(w_hbm.at[:, at], w_ref.at[:, at], w_sem.at[i])

    small = [
        pltpu.make_async_copy(source, target, in_sem.at[i])
        for i, (source, target) in enumerate([
            (q_hbm, q_ref), (qg_hbm, qg_ref), (kg_hbm, kg_ref), (cnt_hbm, cnt_ref),
            (span_hbm, span_ref), (ow_hbm, ow_ref),
        ])
    ]
    for i in range(chunks):
        x_copy(i).start()
        w_copy(i).start()
    for copy in small:
        copy.start()

    barrier = pltpu.get_barrier_semaphore()

    def greet(s, h):
        pl.semaphore_signal(barrier, inc=1, device_id=(s, h), device_id_type=MESH)

    def greet_chain(k, carry):
        greet(2 * lax.rem(place + k, chain) + side, head)
        return carry

    lax.fori_loop(1, chain, greet_chain, 0)
    greet(across, head)
    for level in range(levels):
        greet(seq, partner(level))
    for j in range(ratio):
        for h in range(nh):
            source = ratio * head + j

            @pl.when(jnp.logical_or(source != seq, head != h))
            def _():
                greet(source, h)

    acc[...] = jnp.zeros_like(acc)

    def project(i, carry):
        x_copy(i).wait()
        w_copy(i).wait()
        at = pl.ds(pl.multiple_of(i * CHUNK, CHUNK), CHUNK)
        acc[0:vis, :] += dot(x_ref[:, at], w_ref[:, at], NT)
        return carry

    lax.fori_loop(0, chunks, project, 0)
    raw = acc[...]
    lane = lax.broadcasted_iota(jnp.int32, (1, HD), 1)
    low = lane < HD // 2
    squares = jnp.sum(jnp.where(low, raw * raw, 0.0), axis=1, keepdims=True)
    sq_own[...] = jnp.broadcast_to(squares, sq_own.shape)

    expected = (
        chain + levels + ns
        - jnp.where(seq // ratio == head, 1, 0)
    )
    pl.semaphore_wait(barrier, expected)

    sq_copy = pltpu.make_async_remote_copy(
        src_ref=sq_own, dst_ref=sq_other, send_sem=sq_ss, recv_sem=sq_rs,
        device_id=(seq, mate), device_id_type=MESH,
    )
    sq_copy.start()
    for copy in small[:-1]:
        copy.wait()
    left_half, right_half = [], []
    for h in range(heads_here):
        field = q_ref[:, h * HD : (h + 1) * HD].astype(jnp.float32)
        mean_sq = jnp.mean(field * field, axis=1, keepdims=True)
        normed = field / jnp.sqrt(mean_sq + EPSILON) * qg_ref[...]
        swapped = pltpu.roll(normed, HD // 2, 1)
        left_half.append(jnp.where(low, 0.0, swapped).astype(jnp.bfloat16))
        right_half.append(jnp.where(low, swapped, 0.0).astype(jnp.bfloat16))
    sq_copy.wait()
    inverse = 1.0 / jnp.sqrt((sq_own[...] + sq_other[...]) / HD + EPSILON)
    gain = kg_ref[...]
    gain = jnp.where(core == 0, gain, pltpu.roll(gain, HD // 2, 1))
    block = jnp.where(low, raw * inverse * gain, raw)
    block = jnp.where(core == 0, pltpu.roll(block, HD // 2, 1), block)
    kv[core, seq] = block.astype(jnp.bfloat16)

    def nearest(i):
        both = jnp.minimum(place, chain - 1 - place)
        t = (i + 1) // 2
        near = jnp.where(i % 2 == 1, place - t, place + t)
        far = jnp.where(place < chain - 1 - place, place + (i - both), place - (i - both))
        return jnp.where(i <= 2 * both, near, far)

    def kv_copy(s, kind, target):
        return pltpu.make_async_remote_copy(
            src_ref=kv.at[core, s], dst_ref=kv.at[core, s],
            send_sem=kv_ss.at[s, kind], recv_sem=kv_rs.at[core, s],
            device_id=target, device_id_type=MESH,
        )

    def a_copy(s, kind, target):
        return pltpu.make_async_remote_copy(
            src_ref=att.at[s], dst_ref=att.at[s],
            send_sem=a_ss.at[s, kind], recv_sem=a_rs.at[s],
            device_id=target, device_id_type=MESH,
        )

    def spread(copy, act):
        act(copy(seq, chain, (across, head)))

        def one(i, carry):
            at = nearest(i)
            act(copy(seq, at, (2 * at + side, head)))
            return carry

        lax.fori_loop(1, chain, one, 0)

    def start(copy):
        copy.start()

    def wait_send(copy):
        copy.wait_send()

    slots = jnp.concatenate(
        [jnp.concatenate([left, right], axis=1) for left, right in zip(left_half, right_half)], axis=0
    )
    cap = ns * vis // TILES
    span_f = span_ref[...].astype(jnp.float32)
    first = jnp.transpose(jnp.broadcast_to(span_f[0:1, :], (HD, rows)))[:, 0:1]
    end = jnp.transpose(jnp.broadcast_to(span_f[1:2, :], (HD, rows)))[:, 0:1]
    first = jnp.concatenate([first] * heads_here, axis=0)
    end = jnp.concatenate([end] * heads_here, axis=0)
    scale = math.log2(math.e) / math.sqrt(HD)
    numer[...] = jnp.zeros_like(numer)
    wsum[...] = jnp.zeros_like(wsum)

    def attend(s):
        pltpu.make_async_remote_copy(
            src_ref=kv.at[1 - core, s], dst_ref=kv.at[1 - core, s],
            send_sem=kv_ss.at[s, chain + 1], recv_sem=kv_rs.at[1 - core, s],
            device_id=(seq, mate), device_id_type=MESH,
        ).wait_recv()
        inside = lax.broadcasted_iota(jnp.int32, (1, pad), 1)
        token = inside + s * vis
        tile = jnp.zeros_like(token)
        count = jnp.full_like(token, cnt_ref[0])
        for t in range(1, TILES):
            tile = jnp.where(token >= t * cap, t, tile)
            count = jnp.where(token >= t * cap, t * cap + cnt_ref[t], count)
        present = jnp.logical_and(inside < vis, token < count)
        tile = jnp.where(present, tile, 2 * TILES).astype(jnp.float32)
        allowed = jnp.logical_and(first <= tile, tile < end)
        both = jnp.concatenate([kv[0, s], kv[1, s]], axis=1)
        weights = jnp.where(allowed, jnp.exp2(dot(slots, both, NT) * scale), 0.0)
        wsum[...] += weights
        numer[...] += dot(weights.astype(jnp.bfloat16), both)

    spread(kv_copy, start)
    kv_copy(seq, chain + 1, (seq, mate)).start()

    def kv_step(i, carry):
        @pl.when(jnp.logical_and(i > 0, i < chain))
        def _():
            s = 2 * nearest(i) + side
            kv_copy(s, chain, (across, head)).wait_recv()
            kv_copy(s, chain, (across, head)).start()
            kv_copy(s, chain + 1, (seq, mate)).start()

        @pl.when(jnp.logical_and(i > 0, i <= chain))
        def _():
            attend(2 * nearest(i - 1) + side)
            s = 2 * nearest(i - 1) + 1 - side
            kv_copy(s, chain + 1, (seq, mate)).wait_recv()
            kv_copy(s, chain + 1, (seq, mate)).start()

        @pl.when(i > 1)
        def _():
            attend(2 * nearest(i - 2) + 1 - side)

        return carry

    lax.fori_loop(1, chain + 2, kv_step, 0)
    for h in range(heads_here):
        at = slice(h * rows, (h + 1) * rows)
        total = jnp.sum(wsum[at], axis=1, keepdims=True)
        mixed = jnp.where(low, numer[at, :HD], numer[at, HD:])
        att[seq, :, h * HD : (h + 1) * HD] = (mixed / total).astype(jnp.bfloat16)
    small[-1].wait()
    spread(a_copy, start)

    def level_refs(level):
        if level == 0:
            return send0, recv0
        return sends[level - 1], recvs[level - 1]

    def level_copy(level, s):
        source, target = level_refs(level)
        return pltpu.make_async_remote_copy(
            src_ref=source.at[s], dst_ref=target.at[s],
            send_sem=l_ss.at[level, s], recv_sem=l_rs.at[level, s],
            device_id=(seq, partner(level)), device_id_type=MESH,
        )

    def final_copy(s):
        return pltpu.make_async_remote_copy(
            src_ref=fin.at[s], dst_ref=pieces.at[seq % ratio, head],
            send_sem=f_ss.at[s], recv_sem=f_rs.at[seq % ratio, head],
            device_id=(s, seq // ratio), device_id_type=MESH,
        )

    def is_mine(s):
        return jnp.logical_and(s == seq, seq // ratio == head)

    def turn(i):
        chained = jnp.where(i == 0, 0, (i + 1) // 2)
        swapped = jnp.where(i == ns - 1, chain - 1, jnp.maximum(i // 2 - 1, 0))
        own_side = jnp.logical_or(i == 0, jnp.logical_and(i % 2 == 1, i < ns - 1))
        at = nearest(jnp.where(own_side, chained, swapped))
        return 2 * at + jnp.where(own_side, side, 1 - side), own_side

    sizes = [rows] + [rows >> level for level in range(1, levels)]

    def kept_at(level):
        off = 0
        for done in range(1, level + 1):
            off = off + bit(done) * sizes[done]
        return off

    def first_stage(i):
        s, own_side = turn(i)

        @pl.when(i > 0)
        def _():
            a_copy(s, chain, (across, head)).wait_recv()

        @pl.when(jnp.logical_and(own_side, i > 0))
        def _():
            a_copy(s, chain, (across, head)).start()

        rows_in = att[s]
        other = pl.ds(pl.multiple_of((1 - core) * half, half), half)
        send0[s] = dot(rows_in, ow_ref[:, other]).astype(jnp.bfloat16)
        level_copy(0, s).start()
        mine = pl.ds(pl.multiple_of(core * half, half), half)
        keep[s] = dot(rows_in, ow_ref[:, mine])

    def later_stage(level, i):
        s, _ = turn(i)
        level_copy(level - 1, s).wait_recv()
        size = sizes[level - 1]
        base = kept_at(level - 1)
        arrived = level_refs(level - 1)[1]
        if level == levels:
            total = keep[s, pl.ds(pl.multiple_of(base, size), size)] + arrived[s].astype(jnp.float32)
            fin[s] = total.astype(jnp.bfloat16)

            @pl.when(is_mine(s))
            def _():
                pieces[seq % ratio, head] = fin[s]

            @pl.when(jnp.logical_not(is_mine(s)))
            def _():
                final_copy(s).start()

        else:
            step = sizes[level]
            out_off = (1 - bit(level)) * step
            in_off = bit(level) * step
            sent = keep[s, pl.ds(pl.multiple_of(base + out_off, step), step)]
            sent = sent + arrived[s, pl.ds(pl.multiple_of(out_off, step), step)].astype(jnp.float32)
            level_refs(level)[0][s] = sent.astype(jnp.bfloat16)
            level_copy(level, s).start()
            at = pl.ds(pl.multiple_of(base + in_off, step), step)
            keep[s, at] = keep[s, at] + arrived[s, pl.ds(pl.multiple_of(in_off, step), step)].astype(jnp.float32)

    def pipeline(i, carry):
        @pl.when(i == 1)
        def _():
            later_stage(1, 0)

        @pl.when(i < ns)
        def _():
            first_stage(i)

        @pl.when(jnp.logical_and(i >= 2, i - 1 < ns))
        def _():
            later_stage(1, i - 1)

        for level in range(2, levels + 1):
            lag = 2 * level - 1

            @pl.when(jnp.logical_and(i >= lag, i - lag < ns))
            def _():
                later_stage(level, i - lag)

        return carry

    lax.fori_loop(0, ns + 2 * levels - 1, pipeline, 0)

    for b in range(ratio):
        for h in range(nh):
            @pl.when(jnp.logical_or(ratio * head + b != seq, head != h))
            def _():
                pltpu.make_async_remote_copy(
                    src_ref=fin.at[0], dst_ref=pieces.at[b, h],
                    send_sem=f_ss.at[0], recv_sem=f_rs.at[b, h],
                    device_id=(across, head), device_id_type=MESH,
                ).wait_recv()

            off = sum(((h >> level) & 1) * sizes[level] for level in range(1, levels))
            col = b * 2 * half + (h & 1) * half
            out_ref[off : off + sizes[-1], col : col + half] = pieces[b, h]

    def finish(s, carry):
        @pl.when(jnp.logical_and(s % 2 == side, s != seq))
        def _():
            kv_copy(s, chain, (across, head)).wait_send()
            a_copy(s, chain, (across, head)).wait_send()

        kv_copy(s, chain + 1, (seq, mate)).wait_send()
        for level in range(levels):
            level_copy(level, s).wait_send()

        @pl.when(jnp.logical_not(is_mine(s)))
        def _():
            final_copy(s).wait_send()

        return carry

    lax.fori_loop(0, ns, finish, 0)
    spread(kv_copy, wait_send)
    spread(a_copy, wait_send)


def local(queries, vision, kv_weight, out_weight, q_gain, k_gain, tile_counts, spans):
    ns, nh = lax.axis_size("seq"), lax.axis_size("head")
    rows, width = queries.shape
    vis, model = vision.shape
    cols = out_weight.shape[1]
    half = cols // 2
    levels = int(math.log2(nh))
    pad = -(-vis // 16) * 16
    weights = jnp.swapaxes(kv_weight, 1, 2).reshape(-1, model)
    bf16, f32 = jnp.bfloat16, jnp.float32
    halved = [pltpu.VMEM((ns, rows >> level, half), bf16) for level in range(1, levels)]
    last = rows >> (levels - 1)
    vmem = pl.BlockSpec(memory_space=pltpu.VMEM)
    dma = pltpu.SemaphoreType.DMA
    return pl.pallas_call(
        functools.partial(kernel, ns, nh),
        out_shape=jax.ShapeDtypeStruct((rows, model // nh), bf16),
        in_specs=[pl.BlockSpec(memory_space=pltpu.HBM)] * 8,
        out_specs=vmem,
        scratch_shapes=[
            pltpu.VMEM((rows, width), bf16),
            pltpu.VMEM((vis, model), bf16),
            pltpu.VMEM((HD, model), bf16),
            pltpu.VMEM((width, cols), bf16),
            pltpu.VMEM((1, HD), f32),
            pltpu.VMEM((1, HD), f32),
            pltpu.SMEM((TILES,), jnp.int32),
            pltpu.VMEM((2, rows), jnp.int32),
            dma((6,)), dma((model // CHUNK,)), dma((model // CHUNK,)),
            pltpu.VMEM((rows * width // HD, 2 * HD), f32),
            pltpu.VMEM((rows * width // HD, pad), f32),
            pltpu.VMEM((pad, HD), f32),
            pltpu.VMEM((pad, HD), f32),
            pltpu.VMEM((pad, HD), f32),
            pltpu.VMEM((2, ns, pad, HD), bf16),
            pltpu.VMEM((ns, rows, width), bf16),
            pltpu.VMEM((ns, rows, half), f32),
            pltpu.VMEM((ns, rows, half), bf16),
            pltpu.VMEM((ns, rows, half), bf16),
            halved,
            list(halved),
            pltpu.VMEM((ns, last, half), bf16),
            pltpu.VMEM((ns // nh, nh, last, half), bf16),
            dma, dma, dma((ns, ns // 2 + 2)), dma((2, ns)), dma((ns, ns // 2 + 1)), dma((ns,)),
            dma((levels, ns)), dma((levels, ns)), dma((ns,)), dma((ns // nh, nh)),
        ],
        compiler_params=pltpu.CompilerParams(
            collective_id=0, has_side_effects=True, vmem_limit_bytes=60 * 2**20
        ),
    )(
        queries, vision, weights, out_weight, q_gain.reshape(1, HD), k_gain.reshape(1, HD),
        tile_counts, jnp.swapaxes(spans, 0, 1),
    )


def solution(mesh):
    return jax.shard_map(
        local,
        mesh=mesh,
        in_specs=(
            P("seq", "head"),
            P("seq", None),
            P(None, None, "head"),
            P("head", "seq"),
            P(),
            P(),
            P(),
            P("seq", None),
        ),
        out_specs=P("seq", "head"),
        check_vma=False,
    )
```

```python
import functools
import math

import jax
import jax.numpy as jnp
from jax import lax
from jax.experimental import pallas as pl
from jax.experimental.pallas import tpu as pltpu
from jax.sharding import PartitionSpec as P

HD = 128
TILES = 4
EPSILON = 1e-05
MESH = pl.DeviceIdType.MESH
NT = (((1,), (1,)), ((), ()))
NN = (((1,), (0,)), ((), ()))
CHUNK = 1024


def dot(x, y, dims=NN):
    return lax.dot_general(x, y, dims, preferred_element_type=jnp.float32)


def kernel(
    ns, nh, q_hbm, x_hbm, w_hbm, ow_hbm, qg_hbm, kg_hbm, cnt_hbm, span_hbm, out_ref,
    q_ref, x_ref, w_ref, ow_ref, qg_ref, kg_ref, cnt_ref, span_ref, in_sem, x_sem, w_sem,
    numer, wsum, acc, sq_own, sq_other, kv, att, keep, send0, recv0, sends, recvs, fin, middle, pieces,
    sq_ss, sq_rs, kv_ss, kv_rs, a_ss, a_rs, l_ss, l_rs, f_ss, f_rs, p_ss, p_rs,
):
    seq = lax.axis_index("seq")
    head = lax.axis_index("head")
    ratio = ns // nh
    levels = int(math.log2(nh))
    chain = ns // 2
    place, side = seq // 2, seq % 2
    core = head % 2
    rows = q_ref.shape[0]
    heads_here = q_ref.shape[1] // HD
    vis = x_ref.shape[0]
    pad = kv.shape[2]
    half = ow_ref.shape[1] // 2
    mate = head + 1 - 2 * core
    across = seq + 1 - 2 * side

    def bit(level):
        return (head // 2**level) % 2

    def partner(level):
        return head + 2**level * (1 - 2 * bit(level))

    chunks = x_ref.shape[1] // CHUNK

    def x_copy(i):
        at = pl.ds(pl.multiple_of(i * CHUNK, CHUNK), CHUNK)
        return pltpu.make_async_copy(x_hbm.at[:, at], x_ref.at[:, at], x_sem.at[i])

    def w_copy(i):
        at = pl.ds(pl.multiple_of(i * CHUNK, CHUNK), CHUNK)
        return pltpu.make_async_copy(w_hbm.at[:, at], w_ref.at[:, at], w_sem.at[i])

    small = [
        pltpu.make_async_copy(source, target, in_sem.at[i])
        for i, (source, target) in enumerate([
            (q_hbm, q_ref), (qg_hbm, qg_ref), (kg_hbm, kg_ref), (cnt_hbm, cnt_ref),
            (span_hbm, span_ref), (ow_hbm, ow_ref),
        ])
    ]
    for i in range(chunks):
        x_copy(i).start()
        w_copy(i).start()
    for copy in small:
        copy.start()

    barrier = pltpu.get_barrier_semaphore()

    def greet(s, h):
        pl.semaphore_signal(barrier, inc=1, device_id=(s, h), device_id_type=MESH)

    def greet_chain(k, carry):
        greet(2 * lax.rem(place + k, chain) + side, head)
        return carry

    lax.fori_loop(1, chain, greet_chain, 0)
    greet(across, head)
    for level in range(levels):
        greet(seq, partner(level))
    def greet_sources(k, carry):
        owner, rest = k // ratio, k % ratio
        source = ratio * (2 * owner + core) + rest
        for h in range(2):
            @pl.when(jnp.logical_or(source != seq, core != h))
            def _():
                greet(source, head - core + h)

        return carry

    lax.fori_loop(0, ns // 2, greet_sources, 0)

    def greet_same_core(k, carry):
        greet(seq, lax.rem(head + 2 * k, nh))
        return carry

    lax.fori_loop(1, nh // 2, greet_same_core, 0)

    acc[...] = jnp.zeros_like(acc)

    def project(i, carry):
        x_copy(i).wait()
        w_copy(i).wait()
        at = pl.ds(pl.multiple_of(i * CHUNK, CHUNK), CHUNK)
        acc[0:vis, :] += dot(x_ref[:, at], w_ref[:, at], NT)
        return carry

    lax.fori_loop(0, chunks, project, 0)
    raw = acc[...]
    lane = lax.broadcasted_iota(jnp.int32, (1, HD), 1)
    low = lane < HD // 2
    squares = jnp.sum(jnp.where(low, raw * raw, 0.0), axis=1, keepdims=True)
    sq_own[...] = jnp.broadcast_to(squares, sq_own.shape)

    expected = (
        chain + levels + ns + nh // 2 - 1
        - jnp.where((seq // ratio) % 2 == core, 1, 0)
    )
    pl.semaphore_wait(barrier, expected)

    sq_copy = pltpu.make_async_remote_copy(
        src_ref=sq_own, dst_ref=sq_other, send_sem=sq_ss, recv_sem=sq_rs,
        device_id=(seq, mate), device_id_type=MESH,
    )
    sq_copy.start()
    for copy in small[:-1]:
        copy.wait()
    left_half, right_half = [], []
    for h in range(heads_here):
        field = q_ref[:, h * HD : (h + 1) * HD].astype(jnp.float32)
        mean_sq = jnp.mean(field * field, axis=1, keepdims=True)
        normed = field / jnp.sqrt(mean_sq + EPSILON) * qg_ref[...]
        swapped = pltpu.roll(normed, HD // 2, 1)
        left_half.append(jnp.where(low, 0.0, swapped).astype(jnp.bfloat16))
        right_half.append(jnp.where(low, swapped, 0.0).astype(jnp.bfloat16))
    sq_copy.wait()
    inverse = 1.0 / jnp.sqrt((sq_own[...] + sq_other[...]) / HD + EPSILON)
    gain = kg_ref[...]
    gain = jnp.where(core == 0, gain, pltpu.roll(gain, HD // 2, 1))
    block = jnp.where(low, raw * inverse * gain, raw)
    block = jnp.where(core == 0, pltpu.roll(block, HD // 2, 1), block)
    kv[core, seq] = block.astype(jnp.bfloat16)

    mid = chain // 2
    low_half = place < mid
    gate = jnp.where(low_half, mid - 1, mid)
    other_gate = jnp.where(low_half, mid, mid - 1)
    base_here = jnp.where(low_half, 0, mid)

    def nearest(i):
        crossed = jnp.where(low_half, mid + i - 1, mid - i)
        rest = base_here + (i - mid - 1)
        rest = jnp.where(rest >= place, rest + 1, rest)
        return jnp.where(i == 0, place, jnp.where(i <= mid, crossed, rest))

    def kv_copy(s, kind, target):
        return pltpu.make_async_remote_copy(
            src_ref=kv.at[core, s], dst_ref=kv.at[core, s],
            send_sem=kv_ss.at[s, kind], recv_sem=kv_rs.at[core, s],
            device_id=target, device_id_type=MESH,
        )

    def a_copy(s, kind, target):
        return pltpu.make_async_remote_copy(
            src_ref=att.at[s], dst_ref=att.at[s],
            send_sem=a_ss.at[s, kind], recv_sem=a_rs.at[s],
            device_id=target, device_id_type=MESH,
        )

    def spread(copy, act):
        act(copy(seq, chain, (across, head)))

        def one(i, carry):
            at = nearest(i)
            act(copy(seq, at, (2 * at + side, head)))
            return carry

        lax.fori_loop(1, chain, one, 0)

    def start(copy):
        copy.start()

    def wait_send(copy):
        copy.wait_send()

    def to_own_half(s, act):
        def one(k, carry):
            at = base_here + lax.rem(place - base_here + k, mid)
            act(a_copy(s, at, (2 * at + side, head)))
            return carry

        lax.fori_loop(1, mid, one, 0)

    def spread_attended(act):
        act(a_copy(seq, other_gate, (2 * other_gate + side, head)))
        act(a_copy(seq, chain, (across, head)))
        to_own_half(seq, act)

    def forwards(s):
        return jnp.logical_and(place == gate, (s // 2 < mid) != low_half)

    slots = jnp.concatenate(
        [jnp.concatenate([left, right], axis=1) for left, right in zip(left_half, right_half)], axis=0
    )
    cap = ns * vis // TILES
    span_f = span_ref[...].astype(jnp.float32)
    first = jnp.transpose(jnp.broadcast_to(span_f[0:1, :], (HD, rows)))[:, 0:1]
    end = jnp.transpose(jnp.broadcast_to(span_f[1:2, :], (HD, rows)))[:, 0:1]
    first = jnp.concatenate([first] * heads_here, axis=0)
    end = jnp.concatenate([end] * heads_here, axis=0)
    scale = math.log2(math.e) / math.sqrt(HD)
    numer[...] = jnp.zeros_like(numer)
    wsum[...] = jnp.zeros_like(wsum)

    def attend(s):
        pltpu.make_async_remote_copy(
            src_ref=kv.at[1 - core, s], dst_ref=kv.at[1 - core, s],
            send_sem=kv_ss.at[s, chain + 1], recv_sem=kv_rs.at[1 - core, s],
            device_id=(seq, mate), device_id_type=MESH,
        ).wait_recv()
        inside = lax.broadcasted_iota(jnp.int32, (1, pad), 1)
        token = inside + s * vis
        tile = jnp.zeros_like(token)
        count = jnp.full_like(token, cnt_ref[0])
        for t in range(1, TILES):
            tile = jnp.where(token >= t * cap, t, tile)
            count = jnp.where(token >= t * cap, t * cap + cnt_ref[t], count)
        present = jnp.logical_and(inside < vis, token < count)
        tile = jnp.where(present, tile, 2 * TILES).astype(jnp.float32)
        allowed = jnp.logical_and(first <= tile, tile < end)
        both = jnp.concatenate([kv[0, s], kv[1, s]], axis=1)
        weights = jnp.where(allowed, jnp.exp2(dot(slots, both, NT) * scale), 0.0)
        wsum[...] += weights
        numer[...] += dot(weights.astype(jnp.bfloat16), both)

    spread(kv_copy, start)
    kv_copy(seq, chain + 1, (seq, mate)).start()

    def kv_step(i, carry):
        @pl.when(jnp.logical_and(i > 0, i < chain))
        def _():
            s = 2 * nearest(i) + side
            kv_copy(s, chain, (across, head)).wait_recv()
            kv_copy(s, chain, (across, head)).start()
            kv_copy(s, chain + 1, (seq, mate)).start()

        @pl.when(jnp.logical_and(i > 0, i <= chain))
        def _():
            attend(2 * nearest(i - 1) + side)
            s = 2 * nearest(i - 1) + 1 - side
            kv_copy(s, chain + 1, (seq, mate)).wait_recv()
            kv_copy(s, chain + 1, (seq, mate)).start()

        @pl.when(i > 1)
        def _():
            attend(2 * nearest(i - 2) + 1 - side)

        return carry

    lax.fori_loop(1, chain + 2, kv_step, 0)
    for h in range(heads_here):
        at = slice(h * rows, (h + 1) * rows)
        total = jnp.sum(wsum[at], axis=1, keepdims=True)
        mixed = jnp.where(low, numer[at, :HD], numer[at, HD:])
        att[seq, :, h * HD : (h + 1) * HD] = (mixed / total).astype(jnp.bfloat16)
    small[-1].wait()
    spread_attended(start)

    def level_refs(level):
        if level == 0:
            return send0, recv0
        return sends[level - 1], recvs[level - 1]

    def level_copy(level, s):
        source, target = level_refs(level)
        return pltpu.make_async_remote_copy(
            src_ref=source.at[s], dst_ref=target.at[s],
            send_sem=l_ss.at[level, s], recv_sem=l_rs.at[level, s],
            device_id=(seq, partner(level)), device_id_type=MESH,
        )

    lands = head - core + (seq // ratio) % 2

    def final_copy(s):
        return pltpu.make_async_remote_copy(
            src_ref=fin.at[s], dst_ref=middle.at[seq, core],
            send_sem=f_ss.at[s], recv_sem=f_rs.at[seq, core],
            device_id=(s, lands), device_id_type=MESH,
        )

    def is_mine(s):
        return jnp.logical_and(s == seq, (seq // ratio) % 2 == core)

    def middle_wait(s, c):
        pltpu.make_async_remote_copy(
            src_ref=fin.at[s], dst_ref=middle.at[s, c],
            send_sem=f_ss.at[s], recv_sem=f_rs.at[s, c],
            device_id=(across, head), device_id_type=MESH,
        ).wait_recv()

    def last_copy(s, c):
        return pltpu.make_async_remote_copy(
            src_ref=middle.at[s, c], dst_ref=pieces.at[s % ratio, head - core + c],
            send_sem=p_ss.at[s, c], recv_sem=p_rs.at[s % ratio, head - core + c],
            device_id=(seq, s // ratio), device_id_type=MESH,
        )

    def passes(s):
        return jnp.logical_and((s // ratio) % 2 == core, s // ratio != head)

    def pass_on(i):
        s, _ = turn(i)

        @pl.when((s // ratio) % 2 == core)
        def _():
            for c in range(2):
                @pl.when(jnp.logical_or(s != seq, core != c))
                def _():
                    middle_wait(s, c)

        @pl.when(passes(s))
        def _():
            for c in range(2):
                last_copy(s, c).start()

    def turn(i):
        chained = jnp.where(i == 0, 0, (i + 1) // 2)
        swapped = jnp.where(i == ns - 1, chain - 1, jnp.maximum(i // 2 - 1, 0))
        own_side = jnp.logical_or(i == 0, jnp.logical_and(i % 2 == 1, i < ns - 1))
        at = nearest(jnp.where(own_side, chained, swapped))
        return 2 * at + jnp.where(own_side, side, 1 - side), own_side

    sizes = [rows] + [rows >> level for level in range(1, levels)]

    def kept_at(level):
        off = 0
        for done in range(1, level + 1):
            off = off + bit(done) * sizes[done]
        return off

    def first_stage(i):
        s, own_side = turn(i)

        @pl.when(i > 0)
        def _():
            a_copy(s, chain, (across, head)).wait_recv()

        @pl.when(jnp.logical_and(own_side, i > 0))
        def _():
            @pl.when(forwards(s))
            def _():
                to_own_half(s, start)

            a_copy(s, chain, (across, head)).start()

        rows_in = att[s]
        other = pl.ds(pl.multiple_of((1 - core) * half, half), half)
        send0[s] = dot(rows_in, ow_ref[:, other]).astype(jnp.bfloat16)
        level_copy(0, s).start()
        mine = pl.ds(pl.multiple_of(core * half, half), half)
        keep[s] = dot(rows_in, ow_ref[:, mine])

    def later_stage(level, i):
        s, _ = turn(i)
        level_copy(level - 1, s).wait_recv()
        size = sizes[level - 1]
        base = kept_at(level - 1)
        arrived = level_refs(level - 1)[1]
        if level == levels:
            total = keep[s, pl.ds(pl.multiple_of(base, size), size)] + arrived[s].astype(jnp.float32)
            fin[s] = total.astype(jnp.bfloat16)

            @pl.when(is_mine(s))
            def _():
                middle[seq, core] = fin[s]

            @pl.when(jnp.logical_not(is_mine(s)))
            def _():
                final_copy(s).start()

        else:
            step = sizes[level]
            out_off = (1 - bit(level)) * step
            in_off = bit(level) * step
            sent = keep[s, pl.ds(pl.multiple_of(base + out_off, step), step)]
            sent = sent + arrived[s, pl.ds(pl.multiple_of(out_off, step), step)].astype(jnp.float32)
            level_refs(level)[0][s] = sent.astype(jnp.bfloat16)
            level_copy(level, s).start()
            at = pl.ds(pl.multiple_of(base + in_off, step), step)
            keep[s, at] = keep[s, at] + arrived[s, pl.ds(pl.multiple_of(in_off, step), step)].astype(jnp.float32)

    def pipeline(i, carry):
        @pl.when(i == 1)
        def _():
            later_stage(1, 0)

        @pl.when(i < ns)
        def _():
            first_stage(i)

        @pl.when(jnp.logical_and(i >= 2, i - 1 < ns))
        def _():
            later_stage(1, i - 1)

        for level in range(2, levels + 1):
            lag = 2 * level - 1

            @pl.when(jnp.logical_and(i >= lag, i - lag < ns))
            def _():
                later_stage(level, i - lag)

        @pl.when(i >= 2 * levels + 1)
        def _():
            pass_on(i - 2 * levels - 1)

        return carry

    lax.fori_loop(0, ns + 2 * levels + 1, pipeline, 0)

    for b in range(ratio):
        for h in range(nh):
            off = sum(((h >> level) & 1) * sizes[level] for level in range(1, levels))
            col = b * 2 * half + (h & 1) * half

            @pl.when(head // 2 == h // 2)
            def _():
                out_ref[off : off + sizes[-1], col : col + half] = middle[ratio * head + b, h % 2]

            @pl.when(head // 2 != h // 2)
            def _():
                pltpu.make_async_remote_copy(
                    src_ref=middle.at[0, 0], dst_ref=pieces.at[b, h],
                    send_sem=p_ss.at[0, 0], recv_sem=p_rs.at[b, h],
                    device_id=(across, head), device_id_type=MESH,
                ).wait_recv()
                out_ref[off : off + sizes[-1], col : col + half] = pieces[b, h]

    def finish(s, carry):
        @pl.when(jnp.logical_and(s % 2 == side, s != seq))
        def _():
            kv_copy(s, chain, (across, head)).wait_send()
            a_copy(s, chain, (across, head)).wait_send()

            @pl.when(forwards(s))
            def _():
                to_own_half(s, wait_send)

        kv_copy(s, chain + 1, (seq, mate)).wait_send()
        for level in range(levels):
            level_copy(level, s).wait_send()

        @pl.when(jnp.logical_not(is_mine(s)))
        def _():
            final_copy(s).wait_send()

        @pl.when(passes(s))
        def _():
            for c in range(2):
                last_copy(s, c).wait_send()

        return carry

    lax.fori_loop(0, ns, finish, 0)
    spread(kv_copy, wait_send)
    spread_attended(wait_send)


def local(queries, vision, kv_weight, out_weight, q_gain, k_gain, tile_counts, spans):
    ns, nh = lax.axis_size("seq"), lax.axis_size("head")
    rows, width = queries.shape
    vis, model = vision.shape
    cols = out_weight.shape[1]
    half = cols // 2
    levels = int(math.log2(nh))
    pad = -(-vis // 16) * 16
    weights = jnp.swapaxes(kv_weight, 1, 2).reshape(-1, model)
    bf16, f32 = jnp.bfloat16, jnp.float32
    halved = [pltpu.VMEM((ns, rows >> level, half), bf16) for level in range(1, levels)]
    last = rows >> (levels - 1)
    vmem = pl.BlockSpec(memory_space=pltpu.VMEM)
    dma = pltpu.SemaphoreType.DMA
    return pl.pallas_call(
        functools.partial(kernel, ns, nh),
        out_shape=jax.ShapeDtypeStruct((rows, model // nh), bf16),
        in_specs=[pl.BlockSpec(memory_space=pltpu.HBM)] * 8,
        out_specs=vmem,
        scratch_shapes=[
            pltpu.VMEM((rows, width), bf16),
            pltpu.VMEM((vis, model), bf16),
            pltpu.VMEM((HD, model), bf16),
            pltpu.VMEM((width, cols), bf16),
            pltpu.VMEM((1, HD), f32),
            pltpu.VMEM((1, HD), f32),
            pltpu.SMEM((TILES,), jnp.int32),
            pltpu.VMEM((2, rows), jnp.int32),
            dma((6,)), dma((model // CHUNK,)), dma((model // CHUNK,)),
            pltpu.VMEM((rows * width // HD, 2 * HD), f32),
            pltpu.VMEM((rows * width // HD, pad), f32),
            pltpu.VMEM((pad, HD), f32),
            pltpu.VMEM((pad, HD), f32),
            pltpu.VMEM((pad, HD), f32),
            pltpu.VMEM((2, ns, pad, HD), bf16),
            pltpu.VMEM((ns, rows, width), bf16),
            pltpu.VMEM((ns, rows, half), f32),
            pltpu.VMEM((ns, rows, half), bf16),
            pltpu.VMEM((ns, rows, half), bf16),
            halved,
            list(halved),
            pltpu.VMEM((ns, last, half), bf16),
            pltpu.VMEM((ns, 2, last, half), bf16),
            pltpu.VMEM((ns // nh, nh, last, half), bf16),
            dma, dma, dma((ns, ns // 2 + 2)), dma((2, ns)), dma((ns, ns // 2 + 1)), dma((ns,)),
            dma((levels, ns)), dma((levels, ns)), dma((ns,)), dma((ns, 2)), dma((ns, 2)),
            dma((ns // nh, nh)),
        ],
        compiler_params=pltpu.CompilerParams(
            collective_id=0, has_side_effects=True, vmem_limit_bytes=60 * 2**20
        ),
    )(
        queries, vision, weights, out_weight, q_gain.reshape(1, HD), k_gain.reshape(1, HD),
        tile_counts, jnp.swapaxes(spans, 0, 1),
    )


def solution(mesh):
    return jax.shard_map(
        local,
        mesh=mesh,
        in_specs=(
            P("seq", "head"),
            P("seq", None),
            P(None, None, "head"),
            P("head", "seq"),
            P(),
            P(),
            P(),
            P("seq", None),
        ),
        out_specs=P("seq", "head"),
        check_vma=False,
    )
```

```python
import functools
import math

import jax
import jax.numpy as jnp
from jax import lax
from jax.experimental import pallas as pl
from jax.experimental.pallas import tpu as pltpu
from jax.sharding import PartitionSpec as P

HD = 128
TILES = 4
EPSILON = 1e-05
MESH = pl.DeviceIdType.MESH
NT = (((1,), (1,)), ((), ()))
NN = (((1,), (0,)), ((), ()))
CHUNK = 2048


def dot(x, y, dims=NN):
    return lax.dot_general(x, y, dims, preferred_element_type=jnp.float32)


def kernel(
    ns, nh, q_hbm, x_hbm, w_hbm, ow_hbm, qg_hbm, kg_hbm, cnt_hbm, span_hbm, out_ref,
    q_ref, x_ref, w_ref, ow_ref, qg_ref, kg_ref, cnt_ref, span_ref, in_sem, x_sem, w_sem,
    numer, wsum, acc, sq_own, sq_other, kv, att, keep, send0, recv0, sends, recvs, fin, pieces,
    sq_ss, sq_rs, kv_ss, kv_rs, a_ss, a_rs, l_ss, l_rs, f_ss, f_rs,
):
    seq = lax.axis_index("seq")
    head = lax.axis_index("head")
    ratio = ns // nh
    levels = int(math.log2(nh))
    chain = ns // 2
    place, side = seq // 2, seq % 2
    core = head % 2
    rows = q_ref.shape[0]
    heads_here = q_ref.shape[1] // HD
    vis = x_ref.shape[0]
    pad = kv.shape[2]
    half = ow_ref.shape[1] // 2
    mate = head + 1 - 2 * core
    across = seq + 1 - 2 * side

    def bit(level):
        return (head // 2**level) % 2

    def partner(level):
        return head + 2**level * (1 - 2 * bit(level))

    chunks = x_ref.shape[1] // CHUNK

    def x_copy(i):
        at = pl.ds(pl.multiple_of(i * CHUNK, CHUNK), CHUNK)
        return pltpu.make_async_copy(x_hbm.at[:, at], x_ref.at[:, at], x_sem.at[i])

    def w_copy(i):
        at = pl.ds(pl.multiple_of(i * CHUNK, CHUNK), CHUNK)
        return pltpu.make_async_copy(w_hbm.at[:, at], w_ref.at[:, at], w_sem.at[i])

    small = [
        pltpu.make_async_copy(source, target, in_sem.at[i])
        for i, (source, target) in enumerate([
            (q_hbm, q_ref), (qg_hbm, qg_ref), (kg_hbm, kg_ref), (cnt_hbm, cnt_ref),
            (span_hbm, span_ref), (ow_hbm, ow_ref),
        ])
    ]
    for i in range(chunks):
        x_copy(i).start()
        w_copy(i).start()
    for copy in small:
        copy.start()

    barrier = pltpu.get_barrier_semaphore()

    def greet(s, h):
        pl.semaphore_signal(barrier, inc=1, device_id=(s, h), device_id_type=MESH)

    def greet_chain(k, carry):
        greet(2 * lax.rem(place + k, chain) + side, head)
        return carry

    lax.fori_loop(1, chain, greet_chain, 0)
    greet(across, head)
    for level in range(levels):
        greet(seq, partner(level))
    for j in range(ratio):
        for h in range(nh):
            source = ratio * head + j

            @pl.when(jnp.logical_or(source != seq, head != h))
            def _():
                greet(source, h)

    acc[...] = jnp.zeros_like(acc)

    def project(i, carry):
        x_copy(i).wait()
        w_copy(i).wait()
        at = pl.ds(pl.multiple_of(i * CHUNK, CHUNK), CHUNK)
        acc[0:vis, :] += dot(x_ref[:, at], w_ref[:, at], NT)
        return carry

    lax.fori_loop(0, chunks, project, 0)
    raw = acc[...]
    lane = lax.broadcasted_iota(jnp.int32, (1, HD), 1)
    low = lane < HD // 2
    squares = jnp.sum(jnp.where(low, raw * raw, 0.0), axis=1, keepdims=True)
    sq_own[...] = jnp.broadcast_to(squares, sq_own.shape)

    expected = (
        chain + levels + ns
        - jnp.where(seq // ratio == head, 1, 0)
    )
    pl.semaphore_wait(barrier, expected)

    sq_copy = pltpu.make_async_remote_copy(
        src_ref=sq_own, dst_ref=sq_other, send_sem=sq_ss, recv_sem=sq_rs,
        device_id=(seq, mate), device_id_type=MESH,
    )
    sq_copy.start()
    for copy in small[:-1]:
        copy.wait()
    left_half, right_half = [], []
    for h in range(heads_here):
        field = q_ref[:, h * HD : (h + 1) * HD].astype(jnp.float32)
        mean_sq = jnp.mean(field * field, axis=1, keepdims=True)
        normed = field / jnp.sqrt(mean_sq + EPSILON) * qg_ref[...]
        swapped = pltpu.roll(normed, HD // 2, 1)
        left_half.append(jnp.where(low, 0.0, swapped).astype(jnp.bfloat16))
        right_half.append(jnp.where(low, swapped, 0.0).astype(jnp.bfloat16))
    sq_copy.wait()
    inverse = 1.0 / jnp.sqrt((sq_own[...] + sq_other[...]) / HD + EPSILON)
    gain = kg_ref[...]
    gain = jnp.where(core == 0, gain, pltpu.roll(gain, HD // 2, 1))
    block = jnp.where(low, raw * inverse * gain, raw)
    block = jnp.where(core == 0, pltpu.roll(block, HD // 2, 1), block)
    kv[core, seq] = block.astype(jnp.bfloat16)

    mid = chain // 2
    low_half = place < mid
    base_here = jnp.where(low_half, 0, mid)

    def nearest(i):
        crossed = jnp.where(low_half, mid + i - 1, mid - i)
        rest = base_here + (i - mid - 1)
        rest = jnp.where(rest >= place, rest + 1, rest)
        return jnp.where(i == 0, place, jnp.where(i <= mid, crossed, rest))

    def kv_copy(s, kind, target):
        return pltpu.make_async_remote_copy(
            src_ref=kv.at[core, s], dst_ref=kv.at[core, s],
            send_sem=kv_ss.at[s, kind], recv_sem=kv_rs.at[core, s],
            device_id=target, device_id_type=MESH,
        )

    def a_copy(s, kind, target):
        return pltpu.make_async_remote_copy(
            src_ref=att.at[s], dst_ref=att.at[s],
            send_sem=a_ss.at[s, kind], recv_sem=a_rs.at[s],
            device_id=target, device_id_type=MESH,
        )

    def spread(copy, act):
        act(copy(seq, chain, (across, head)))

        def one(i, carry):
            at = nearest(i)
            act(copy(seq, at, (2 * at + side, head)))
            return carry

        lax.fori_loop(1, chain, one, 0)

    def start(copy):
        copy.start()

    def wait_send(copy):
        copy.wait_send()

    slots = jnp.concatenate(
        [jnp.concatenate([left, right], axis=1) for left, right in zip(left_half, right_half)], axis=0
    )
    cap = ns * vis // TILES
    span_f = span_ref[...].astype(jnp.float32)
    first = jnp.transpose(jnp.broadcast_to(span_f[0:1, :], (HD, rows)))[:, 0:1]
    end = jnp.transpose(jnp.broadcast_to(span_f[1:2, :], (HD, rows)))[:, 0:1]
    first = jnp.concatenate([first] * heads_here, axis=0)
    end = jnp.concatenate([end] * heads_here, axis=0)
    scale = math.log2(math.e) / math.sqrt(HD)
    numer[...] = jnp.zeros_like(numer)
    wsum[...] = jnp.zeros_like(wsum)

    def attend(s):
        pltpu.make_async_remote_copy(
            src_ref=kv.at[1 - core, s], dst_ref=kv.at[1 - core, s],
            send_sem=kv_ss.at[s, chain + 1], recv_sem=kv_rs.at[1 - core, s],
            device_id=(seq, mate), device_id_type=MESH,
        ).wait_recv()
        inside = lax.broadcasted_iota(jnp.int32, (1, pad), 1)
        token = inside + s * vis
        tile = jnp.zeros_like(token)
        count = jnp.full_like(token, cnt_ref[0])
        for t in range(1, TILES):
            tile = jnp.where(token >= t * cap, t, tile)
            count = jnp.where(token >= t * cap, t * cap + cnt_ref[t], count)
        present = jnp.logical_and(inside < vis, token < count)
        tile = jnp.where(present, tile, 2 * TILES).astype(jnp.float32)
        allowed = jnp.logical_and(first <= tile, tile < end)
        both = jnp.concatenate([kv[0, s], kv[1, s]], axis=1)
        weights = jnp.where(allowed, jnp.exp2(dot(slots, both, NT) * scale), 0.0)
        wsum[...] += weights
        numer[...] += dot(weights.astype(jnp.bfloat16), both)

    spread(kv_copy, start)
    kv_copy(seq, chain + 1, (seq, mate)).start()

    def kv_step(i, carry):
        @pl.when(jnp.logical_and(i > 0, i < chain))
        def _():
            s = 2 * nearest(i) + side
            kv_copy(s, chain, (across, head)).wait_recv()
            kv_copy(s, chain, (across, head)).start()
            kv_copy(s, chain + 1, (seq, mate)).start()

        @pl.when(jnp.logical_and(i > 0, i <= chain))
        def _():
            attend(2 * nearest(i - 1) + side)
            s = 2 * nearest(i - 1) + 1 - side
            kv_copy(s, chain + 1, (seq, mate)).wait_recv()
            kv_copy(s, chain + 1, (seq, mate)).start()

        @pl.when(i > 1)
        def _():
            attend(2 * nearest(i - 2) + 1 - side)

        return carry

    lax.fori_loop(1, chain + 2, kv_step, 0)
    for h in range(heads_here):
        at = slice(h * rows, (h + 1) * rows)
        total = jnp.sum(wsum[at], axis=1, keepdims=True)
        mixed = jnp.where(low, numer[at, :HD], numer[at, HD:])
        att[seq, :, h * HD : (h + 1) * HD] = (mixed / total).astype(jnp.bfloat16)
    small[-1].wait()
    spread(a_copy, start)

    def level_refs(level):
        if level == 0:
            return send0, recv0
        return sends[level - 1], recvs[level - 1]

    def level_copy(level, s):
        source, target = level_refs(level)
        return pltpu.make_async_remote_copy(
            src_ref=source.at[s], dst_ref=target.at[s],
            send_sem=l_ss.at[level, s], recv_sem=l_rs.at[level, s],
            device_id=(seq, partner(level)), device_id_type=MESH,
        )

    def final_copy(s):
        return pltpu.make_async_remote_copy(
            src_ref=fin.at[s], dst_ref=pieces.at[seq % ratio, head],
            send_sem=f_ss.at[s], recv_sem=f_rs.at[seq % ratio, head],
            device_id=(s, seq // ratio), device_id_type=MESH,
        )

    def is_mine(s):
        return jnp.logical_and(s == seq, seq // ratio == head)

    def turn(i):
        chained = jnp.where(i == 0, 0, (i + 1) // 2)
        swapped = jnp.where(i == ns - 1, chain - 1, jnp.maximum(i // 2 - 1, 0))
        own_side = jnp.logical_or(i == 0, jnp.logical_and(i % 2 == 1, i < ns - 1))
        at = nearest(jnp.where(own_side, chained, swapped))
        return 2 * at + jnp.where(own_side, side, 1 - side), own_side

    sizes = [rows] + [rows >> level for level in range(1, levels)]

    def kept_at(level):
        off = 0
        for done in range(1, level + 1):
            off = off + bit(done) * sizes[done]
        return off

    def first_stage(i):
        s, own_side = turn(i)

        @pl.when(i > 0)
        def _():
            a_copy(s, chain, (across, head)).wait_recv()

        @pl.when(jnp.logical_and(own_side, i > 0))
        def _():
            a_copy(s, chain, (across, head)).start()

        rows_in = att[s]
        other = pl.ds(pl.multiple_of((1 - core) * half, half), half)
        send0[s] = dot(rows_in, ow_ref[:, other]).astype(jnp.bfloat16)
        level_copy(0, s).start()
        mine = pl.ds(pl.multiple_of(core * half, half), half)
        keep[s] = dot(rows_in, ow_ref[:, mine])

    def later_stage(level, i):
        s, _ = turn(i)
        level_copy(level - 1, s).wait_recv()
        size = sizes[level - 1]
        base = kept_at(level - 1)
        arrived = level_refs(level - 1)[1]
        if level == levels:
            total = keep[s, pl.ds(pl.multiple_of(base, size), size)] + arrived[s].astype(jnp.float32)
            fin[s] = total.astype(jnp.bfloat16)

            @pl.when(is_mine(s))
            def _():
                pieces[seq % ratio, head] = fin[s]

            @pl.when(jnp.logical_not(is_mine(s)))
            def _():
                final_copy(s).start()

        else:
            step = sizes[level]
            out_off = (1 - bit(level)) * step
            in_off = bit(level) * step
            sent = keep[s, pl.ds(pl.multiple_of(base + out_off, step), step)]
            sent = sent + arrived[s, pl.ds(pl.multiple_of(out_off, step), step)].astype(jnp.float32)
            level_refs(level)[0][s] = sent.astype(jnp.bfloat16)
            level_copy(level, s).start()
            at = pl.ds(pl.multiple_of(base + in_off, step), step)
            keep[s, at] = keep[s, at] + arrived[s, pl.ds(pl.multiple_of(in_off, step), step)].astype(jnp.float32)

    def pipeline(i, carry):
        @pl.when(i == 1)
        def _():
            later_stage(1, 0)

        @pl.when(i < ns)
        def _():
            first_stage(i)

        @pl.when(jnp.logical_and(i >= 2, i - 1 < ns))
        def _():
            later_stage(1, i - 1)

        for level in range(2, levels + 1):
            lag = 2 * level - 1

            @pl.when(jnp.logical_and(i >= lag, i - lag < ns))
            def _():
                later_stage(level, i - lag)

        return carry

    lax.fori_loop(0, ns + 2 * levels - 1, pipeline, 0)

    for b in range(ratio):
        for h in range(nh):
            @pl.when(jnp.logical_or(ratio * head + b != seq, head != h))
            def _():
                pltpu.make_async_remote_copy(
                    src_ref=fin.at[0], dst_ref=pieces.at[b, h],
                    send_sem=f_ss.at[0], recv_sem=f_rs.at[b, h],
                    device_id=(across, head), device_id_type=MESH,
                ).wait_recv()

            off = sum(((h >> level) & 1) * sizes[level] for level in range(1, levels))
            col = b * 2 * half + (h & 1) * half
            out_ref[off : off + sizes[-1], col : col + half] = pieces[b, h]

    def finish(s, carry):
        @pl.when(jnp.logical_and(s % 2 == side, s != seq))
        def _():
            kv_copy(s, chain, (across, head)).wait_send()
            a_copy(s, chain, (across, head)).wait_send()

        kv_copy(s, chain + 1, (seq, mate)).wait_send()
        for level in range(levels):
            level_copy(level, s).wait_send()

        @pl.when(jnp.logical_not(is_mine(s)))
        def _():
            final_copy(s).wait_send()

        return carry

    lax.fori_loop(0, ns, finish, 0)
    spread(kv_copy, wait_send)
    spread(a_copy, wait_send)


def local(queries, vision, kv_weight, out_weight, q_gain, k_gain, tile_counts, spans):
    ns, nh = lax.axis_size("seq"), lax.axis_size("head")
    rows, width = queries.shape
    vis, model = vision.shape
    cols = out_weight.shape[1]
    half = cols // 2
    levels = int(math.log2(nh))
    pad = -(-vis // 16) * 16
    weights = jnp.swapaxes(kv_weight, 1, 2).reshape(-1, model)
    bf16, f32 = jnp.bfloat16, jnp.float32
    halved = [pltpu.VMEM((ns, rows >> level, half), bf16) for level in range(1, levels)]
    last = rows >> (levels - 1)
    vmem = pl.BlockSpec(memory_space=pltpu.VMEM)
    dma = pltpu.SemaphoreType.DMA
    return pl.pallas_call(
        functools.partial(kernel, ns, nh),
        out_shape=jax.ShapeDtypeStruct((rows, model // nh), bf16),
        in_specs=[pl.BlockSpec(memory_space=pltpu.HBM)] * 8,
        out_specs=vmem,
        scratch_shapes=[
            pltpu.VMEM((rows, width), bf16),
            pltpu.VMEM((vis, model), bf16),
            pltpu.VMEM((HD, model), bf16),
            pltpu.VMEM((width, cols), bf16),
            pltpu.VMEM((1, HD), f32),
            pltpu.VMEM((1, HD), f32),
            pltpu.SMEM((TILES,), jnp.int32),
            pltpu.VMEM((2, rows), jnp.int32),
            dma((6,)), dma((model // CHUNK,)), dma((model // CHUNK,)),
            pltpu.VMEM((rows * width // HD, 2 * HD), f32),
            pltpu.VMEM((rows * width // HD, pad), f32),
            pltpu.VMEM((pad, HD), f32),
            pltpu.VMEM((pad, HD), f32),
            pltpu.VMEM((pad, HD), f32),
            pltpu.VMEM((2, ns, pad, HD), bf16),
            pltpu.VMEM((ns, rows, width), bf16),
            pltpu.VMEM((ns, rows, half), f32),
            pltpu.VMEM((ns, rows, half), bf16),
            pltpu.VMEM((ns, rows, half), bf16),
            halved,
            list(halved),
            pltpu.VMEM((ns, last, half), bf16),
            pltpu.VMEM((ns // nh, nh, last, half), bf16),
            dma, dma, dma((ns, ns // 2 + 2)), dma((2, ns)), dma((ns, ns // 2 + 1)), dma((ns,)),
            dma((levels, ns)), dma((levels, ns)), dma((ns,)), dma((ns // nh, nh)),
        ],
        compiler_params=pltpu.CompilerParams(
            collective_id=0, has_side_effects=True, vmem_limit_bytes=60 * 2**20
        ),
    )(
        queries, vision, weights, out_weight, q_gain.reshape(1, HD), k_gain.reshape(1, HD),
        tile_counts, jnp.swapaxes(spans, 0, 1),
    )


def solution(mesh):
    return jax.shard_map(
        local,
        mesh=mesh,
        in_specs=(
            P("seq", "head"),
            P("seq", None),
            P(None, None, "head"),
            P("head", "seq"),
            P(),
            P(),
            P(),
            P("seq", None),
        ),
        out_specs=P("seq", "head"),
        check_vma=False,
    )
```

```python
import functools
import math

import jax
import jax.numpy as jnp
from jax import lax
from jax.experimental import pallas as pl
from jax.experimental.pallas import tpu as pltpu
from jax.sharding import PartitionSpec as P

HD = 128
TILES = 4
EPSILON = 1e-05
MESH = pl.DeviceIdType.MESH
NT = (((1,), (1,)), ((), ()))
NN = (((1,), (0,)), ((), ()))
CHUNK = 1024


def dot(x, y, dims=NN):
    return lax.dot_general(x, y, dims, preferred_element_type=jnp.float32)


def kernel(
    ns, nh, q_hbm, x_hbm, w_hbm, ow_hbm, qg_hbm, kg_hbm, cnt_hbm, span_hbm, out_ref,
    q_ref, x_ref, w_ref, ow_ref, qg_ref, kg_ref, cnt_ref, span_ref, in_sem, x_sem, w_sem,
    numer, wsum, acc, sq_own, sq_other, kv, att, keep, send0, recv0, sends, recvs, fin, pieces,
    sq_ss, sq_rs, kv_ss, kv_rs, a_ss, a_rs, l_ss, l_rs, f_ss, f_rs,
):
    seq = lax.axis_index("seq")
    head = lax.axis_index("head")
    ratio = ns // nh
    levels = int(math.log2(nh))
    chain = ns // 2
    place, side = seq // 2, seq % 2
    core = head % 2
    rows = q_ref.shape[0]
    heads_here = q_ref.shape[1] // HD
    vis = x_ref.shape[0]
    pad = kv.shape[2]
    half = ow_ref.shape[1] // 2
    mate = head + 1 - 2 * core
    across = seq + 1 - 2 * side

    def bit(level):
        return (head // 2**level) % 2

    def partner(level):
        return head + 2**level * (1 - 2 * bit(level))

    chunks = x_ref.shape[1] // CHUNK

    def x_copy(i):
        at = pl.ds(pl.multiple_of(i * CHUNK, CHUNK), CHUNK)
        return pltpu.make_async_copy(x_hbm.at[:, at], x_ref.at[:, at], x_sem.at[i])

    def w_copy(i):
        at = pl.ds(pl.multiple_of(i * CHUNK, CHUNK), CHUNK)
        return pltpu.make_async_copy(w_hbm.at[:, at], w_ref.at[:, at], w_sem.at[i])

    small = [
        pltpu.make_async_copy(source, target, in_sem.at[i])
        for i, (source, target) in enumerate([
            (q_hbm, q_ref), (qg_hbm, qg_ref), (kg_hbm, kg_ref), (cnt_hbm, cnt_ref),
            (span_hbm, span_ref), (ow_hbm, ow_ref),
        ])
    ]
    for i in range(chunks):
        x_copy(i).start()
        w_copy(i).start()
    for copy in small:
        copy.start()

    barrier = pltpu.get_barrier_semaphore()

    def greet(s, h):
        pl.semaphore_signal(barrier, inc=1, device_id=(s, h), device_id_type=MESH)

    def greet_chain(k, carry):
        greet(2 * lax.rem(place + k, chain) + side, head)
        return carry

    lax.fori_loop(1, chain, greet_chain, 0)
    greet(across, head)
    for level in range(levels):
        greet(seq, partner(level))
    for j in range(ratio):
        for h in range(nh):
            source = ratio * head + j

            @pl.when(jnp.logical_or(source != seq, head != h))
            def _():
                greet(source, h)

    acc[...] = jnp.zeros_like(acc)

    def project(i, carry):
        x_copy(i).wait()
        w_copy(i).wait()
        at = pl.ds(pl.multiple_of(i * CHUNK, CHUNK), CHUNK)
        acc[0:vis, :] += dot(x_ref[:, at], w_ref[:, at], NT)
        return carry

    lax.fori_loop(0, chunks, project, 0)
    raw = acc[...]
    lane = lax.broadcasted_iota(jnp.int32, (1, HD), 1)
    low = lane < HD // 2
    squares = jnp.sum(jnp.where(low, raw * raw, 0.0), axis=1, keepdims=True)
    sq_own[...] = jnp.broadcast_to(squares, sq_own.shape)

    expected = (
        chain + levels + ns
        - jnp.where(seq // ratio == head, 1, 0)
    )
    pl.semaphore_wait(barrier, expected)

    sq_copy = pltpu.make_async_remote_copy(
        src_ref=sq_own, dst_ref=sq_other, send_sem=sq_ss, recv_sem=sq_rs,
        device_id=(seq, mate), device_id_type=MESH,
    )
    sq_copy.start()
    for copy in small[:-1]:
        copy.wait()
    left_half, right_half = [], []
    for h in range(heads_here):
        field = q_ref[:, h * HD : (h + 1) * HD].astype(jnp.float32)
        mean_sq = jnp.mean(field * field, axis=1, keepdims=True)
        normed = field / jnp.sqrt(mean_sq + EPSILON) * qg_ref[...]
        swapped = pltpu.roll(normed, HD // 2, 1)
        left_half.append(jnp.where(low, 0.0, swapped).astype(jnp.bfloat16))
        right_half.append(jnp.where(low, swapped, 0.0).astype(jnp.bfloat16))
    sq_copy.wait()
    inverse = 1.0 / jnp.sqrt((sq_own[...] + sq_other[...]) / HD + EPSILON)
    gain = kg_ref[...]
    gain = jnp.where(core == 0, gain, pltpu.roll(gain, HD // 2, 1))
    block = jnp.where(low, raw * inverse * gain, raw)
    block = jnp.where(core == 0, pltpu.roll(block, HD // 2, 1), block)
    kv[core, seq] = block.astype(jnp.bfloat16)

    def nearest(i):
        both = jnp.minimum(place, chain - 1 - place)
        t = (i + 1) // 2
        inward = jnp.where(place < chain // 2, 1, -1)
        near = jnp.where(i % 2 == 1, place + inward * t, place - inward * t)
        far = jnp.where(place < chain - 1 - place, place + (i - both), place - (i - both))
        return jnp.where(i <= 2 * both, near, far)

    def kv_copy(s, kind, target):
        return pltpu.make_async_remote_copy(
            src_ref=kv.at[core, s], dst_ref=kv.at[core, s],
            send_sem=kv_ss.at[s, kind], recv_sem=kv_rs.at[core, s],
            device_id=target, device_id_type=MESH,
        )

    def a_copy(s, kind, target):
        return pltpu.make_async_remote_copy(
            src_ref=att.at[s], dst_ref=att.at[s],
            send_sem=a_ss.at[s, kind], recv_sem=a_rs.at[s],
            device_id=target, device_id_type=MESH,
        )

    def spread(copy, act):
        act(copy(seq, chain, (across, head)))

        def one(i, carry):
            at = nearest(i)
            act(copy(seq, at, (2 * at + side, head)))
            return carry

        lax.fori_loop(1, chain, one, 0)

    def start(copy):
        copy.start()

    def wait_send(copy):
        copy.wait_send()

    slots = jnp.concatenate(
        [jnp.concatenate([left, right], axis=1) for left, right in zip(left_half, right_half)], axis=0
    )
    cap = ns * vis // TILES
    span_f = span_ref[...].astype(jnp.float32)
    first = jnp.transpose(jnp.broadcast_to(span_f[0:1, :], (HD, rows)))[:, 0:1]
    end = jnp.transpose(jnp.broadcast_to(span_f[1:2, :], (HD, rows)))[:, 0:1]
    first = jnp.concatenate([first] * heads_here, axis=0)
    end = jnp.concatenate([end] * heads_here, axis=0)
    scale = math.log2(math.e) / math.sqrt(HD)
    numer[...] = jnp.zeros_like(numer)
    wsum[...] = jnp.zeros_like(wsum)

    def attend(s):
        pltpu.make_async_remote_copy(
            src_ref=kv.at[1 - core, s], dst_ref=kv.at[1 - core, s],
            send_sem=kv_ss.at[s, chain + 1], recv_sem=kv_rs.at[1 - core, s],
            device_id=(seq, mate), device_id_type=MESH,
        ).wait_recv()
        inside = lax.broadcasted_iota(jnp.int32, (1, pad), 1)
        token = inside + s * vis
        tile = jnp.zeros_like(token)
        count = jnp.full_like(token, cnt_ref[0])
        for t in range(1, TILES):
            tile = jnp.where(token >= t * cap, t, tile)
            count = jnp.where(token >= t * cap, t * cap + cnt_ref[t], count)
        present = jnp.logical_and(inside < vis, token < count)
        tile = jnp.where(present, tile, 2 * TILES).astype(jnp.float32)
        allowed = jnp.logical_and(first <= tile, tile < end)
        both = jnp.concatenate([kv[0, s], kv[1, s]], axis=1)
        weights = jnp.where(allowed, jnp.exp2(dot(slots, both, NT) * scale), 0.0)
        wsum[...] += weights
        numer[...] += dot(weights.astype(jnp.bfloat16), both)

    spread(kv_copy, start)
    kv_copy(seq, chain + 1, (seq, mate)).start()

    def kv_step(i, carry):
        @pl.when(jnp.logical_and(i > 0, i < chain))
        def _():
            s = 2 * nearest(i) + side
            kv_copy(s, chain, (across, head)).wait_recv()
            kv_copy(s, chain, (across, head)).start()
            kv_copy(s, chain + 1, (seq, mate)).start()

        @pl.when(jnp.logical_and(i > 0, i <= chain))
        def _():
            attend(2 * nearest(i - 1) + side)
            s = 2 * nearest(i - 1) + 1 - side
            kv_copy(s, chain + 1, (seq, mate)).wait_recv()
            kv_copy(s, chain + 1, (seq, mate)).start()

        @pl.when(i > 1)
        def _():
            attend(2 * nearest(i - 2) + 1 - side)

        return carry

    lax.fori_loop(1, chain + 2, kv_step, 0)
    for h in range(heads_here):
        at = slice(h * rows, (h + 1) * rows)
        total = jnp.sum(wsum[at], axis=1, keepdims=True)
        mixed = jnp.where(low, numer[at, :HD], numer[at, HD:])
        att[seq, :, h * HD : (h + 1) * HD] = (mixed / total).astype(jnp.bfloat16)
    small[-1].wait()
    spread(a_copy, start)

    def level_refs(level):
        if level == 0:
            return send0, recv0
        return sends[level - 1], recvs[level - 1]

    def level_copy(level, s):
        source, target = level_refs(level)
        return pltpu.make_async_remote_copy(
            src_ref=source.at[s], dst_ref=target.at[s],
            send_sem=l_ss.at[level, s], recv_sem=l_rs.at[level, s],
            device_id=(seq, partner(level)), device_id_type=MESH,
        )

    def final_copy(s):
        return pltpu.make_async_remote_copy(
            src_ref=fin.at[s], dst_ref=pieces.at[seq % ratio, head],
            send_sem=f_ss.at[s], recv_sem=f_rs.at[seq % ratio, head],
            device_id=(s, seq // ratio), device_id_type=MESH,
        )

    def is_mine(s):
        return jnp.logical_and(s == seq, seq // ratio == head)

    def turn(i):
        chained = jnp.where(i == 0, 0, (i + 1) // 2)
        swapped = jnp.where(i == ns - 1, chain - 1, jnp.maximum(i // 2 - 1, 0))
        own_side = jnp.logical_or(i == 0, jnp.logical_and(i % 2 == 1, i < ns - 1))
        at = nearest(jnp.where(own_side, chained, swapped))
        return 2 * at + jnp.where(own_side, side, 1 - side), own_side

    sizes = [rows] + [rows >> level for level in range(1, levels)]

    def kept_at(level):
        off = 0
        for done in range(1, level + 1):
            off = off + bit(done) * sizes[done]
        return off

    def first_stage(i):
        s, own_side = turn(i)

        @pl.when(jnp.logical_not(own_side))
        def _():
            a_copy(s, chain, (across, head)).wait_recv()

        rows_in = att[s]
        other = pl.ds(pl.multiple_of((1 - core) * half, half), half)
        send0[s] = dot(rows_in, ow_ref[:, other]).astype(jnp.bfloat16)
        level_copy(0, s).start()
        mine = pl.ds(pl.multiple_of(core * half, half), half)
        keep[s] = dot(rows_in, ow_ref[:, mine])

    def forward(k):
        s = 2 * nearest(k) + side
        a_copy(s, chain, (across, head)).wait_recv()
        a_copy(s, chain, (across, head)).start()

    def later_stage(level, i):
        s, _ = turn(i)
        level_copy(level - 1, s).wait_recv()
        size = sizes[level - 1]
        base = kept_at(level - 1)
        arrived = level_refs(level - 1)[1]
        if level == levels:
            total = keep[s, pl.ds(pl.multiple_of(base, size), size)] + arrived[s].astype(jnp.float32)
            fin[s] = total.astype(jnp.bfloat16)

            @pl.when(is_mine(s))
            def _():
                pieces[seq % ratio, head] = fin[s]

            @pl.when(jnp.logical_not(is_mine(s)))
            def _():
                final_copy(s).start()

        else:
            step = sizes[level]
            out_off = (1 - bit(level)) * step
            in_off = bit(level) * step
            sent = keep[s, pl.ds(pl.multiple_of(base + out_off, step), step)]
            sent = sent + arrived[s, pl.ds(pl.multiple_of(out_off, step), step)].astype(jnp.float32)
            level_refs(level)[0][s] = sent.astype(jnp.bfloat16)
            level_copy(level, s).start()
            at = pl.ds(pl.multiple_of(base + in_off, step), step)
            keep[s, at] = keep[s, at] + arrived[s, pl.ds(pl.multiple_of(in_off, step), step)].astype(jnp.float32)

    def pipeline(i, carry):
        @pl.when(i == 1)
        def _():
            later_stage(1, 0)
            forward(1)

        @pl.when(i < ns)
        def _():
            first_stage(i)

        @pl.when(jnp.logical_and(i % 2 == 0, jnp.logical_and(i >= 2, i < ns - 2)))
        def _():
            forward(i // 2 + 1)

        @pl.when(jnp.logical_and(i >= 2, i - 1 < ns))
        def _():
            later_stage(1, i - 1)

        for level in range(2, levels + 1):
            lag = 2 * level - 1

            @pl.when(jnp.logical_and(i >= lag, i - lag < ns))
            def _():
                later_stage(level, i - lag)

        return carry

    lax.fori_loop(0, ns + 2 * levels - 1, pipeline, 0)

    for b in range(ratio):
        for h in range(nh):
            @pl.when(jnp.logical_or(ratio * head + b != seq, head != h))
            def _():
                pltpu.make_async_remote_copy(
                    src_ref=fin.at[0], dst_ref=pieces.at[b, h],
                    send_sem=f_ss.at[0], recv_sem=f_rs.at[b, h],
                    device_id=(across, head), device_id_type=MESH,
                ).wait_recv()

            off = sum(((h >> level) & 1) * sizes[level] for level in range(1, levels))
            col = b * 2 * half + (h & 1) * half
            out_ref[off : off + sizes[-1], col : col + half] = pieces[b, h]

    def finish(s, carry):
        @pl.when(jnp.logical_and(s % 2 == side, s != seq))
        def _():
            kv_copy(s, chain, (across, head)).wait_send()
            a_copy(s, chain, (across, head)).wait_send()

        kv_copy(s, chain + 1, (seq, mate)).wait_send()
        for level in range(levels):
            level_copy(level, s).wait_send()

        @pl.when(jnp.logical_not(is_mine(s)))
        def _():
            final_copy(s).wait_send()

        return carry

    lax.fori_loop(0, ns, finish, 0)
    spread(kv_copy, wait_send)
    spread(a_copy, wait_send)


def local(queries, vision, kv_weight, out_weight, q_gain, k_gain, tile_counts, spans):
    ns, nh = lax.axis_size("seq"), lax.axis_size("head")
    rows, width = queries.shape
    vis, model = vision.shape
    cols = out_weight.shape[1]
    half = cols // 2
    levels = int(math.log2(nh))
    pad = -(-vis // 16) * 16
    weights = jnp.swapaxes(kv_weight, 1, 2).reshape(-1, model)
    bf16, f32 = jnp.bfloat16, jnp.float32
    halved = [pltpu.VMEM((ns, rows >> level, half), bf16) for level in range(1, levels)]
    last = rows >> (levels - 1)
    vmem = pl.BlockSpec(memory_space=pltpu.VMEM)
    dma = pltpu.SemaphoreType.DMA
    return pl.pallas_call(
        functools.partial(kernel, ns, nh),
        out_shape=jax.ShapeDtypeStruct((rows, model // nh), bf16),
        in_specs=[pl.BlockSpec(memory_space=pltpu.HBM)] * 8,
        out_specs=vmem,
        scratch_shapes=[
            pltpu.VMEM((rows, width), bf16),
            pltpu.VMEM((vis, model), bf16),
            pltpu.VMEM((HD, model), bf16),
            pltpu.VMEM((width, cols), bf16),
            pltpu.VMEM((1, HD), f32),
            pltpu.VMEM((1, HD), f32),
            pltpu.SMEM((TILES,), jnp.int32),
            pltpu.VMEM((2, rows), jnp.int32),
            dma((6,)), dma((model // CHUNK,)), dma((model // CHUNK,)),
            pltpu.VMEM((rows * width // HD, 2 * HD), f32),
            pltpu.VMEM((rows * width // HD, pad), f32),
            pltpu.VMEM((pad, HD), f32),
            pltpu.VMEM((pad, HD), f32),
            pltpu.VMEM((pad, HD), f32),
            pltpu.VMEM((2, ns, pad, HD), bf16),
            pltpu.VMEM((ns, rows, width), bf16),
            pltpu.VMEM((ns, rows, half), f32),
            pltpu.VMEM((ns, rows, half), bf16),
            pltpu.VMEM((ns, rows, half), bf16),
            halved,
            list(halved),
            pltpu.VMEM((ns, last, half), bf16),
            pltpu.VMEM((ns // nh, nh, last, half), bf16),
            dma, dma, dma((ns, ns // 2 + 2)), dma((2, ns)), dma((ns, ns // 2 + 1)), dma((ns,)),
            dma((levels, ns)), dma((levels, ns)), dma((ns,)), dma((ns // nh, nh)),
        ],
        compiler_params=pltpu.CompilerParams(
            collective_id=0, has_side_effects=True, vmem_limit_bytes=60 * 2**20
        ),
    )(
        queries, vision, weights, out_weight, q_gain.reshape(1, HD), k_gain.reshape(1, HD),
        tile_counts, jnp.swapaxes(spans, 0, 1),
    )


def solution(mesh):
    return jax.shard_map(
        local,
        mesh=mesh,
        in_specs=(
            P("seq", "head"),
            P("seq", None),
            P(None, None, "head"),
            P("head", "seq"),
            P(),
            P(),
            P(),
            P("seq", None),
        ),
        out_specs=P("seq", "head"),
        check_vma=False,
    )
```

```python
import functools
import math

import jax
import jax.numpy as jnp
from jax import lax
from jax.experimental import pallas as pl
from jax.experimental.pallas import tpu as pltpu
from jax.sharding import PartitionSpec as P

HD = 128
TILES = 4
EPSILON = 1e-05
MESH = pl.DeviceIdType.MESH
NT = (((1,), (1,)), ((), ()))
NN = (((1,), (0,)), ((), ()))
CHUNK = 1024


def dot(x, y, dims=NN):
    return lax.dot_general(x, y, dims, preferred_element_type=jnp.float32)


def kernel(
    ns, nh, q_hbm, x_hbm, w_hbm, ow_hbm, qg_hbm, kg_hbm, cnt_hbm, span_hbm, out_ref,
    q_ref, x_ref, w_ref, ow_ref, qg_ref, kg_ref, cnt_ref, span_ref, in_sem, x_sem, w_sem,
    numer, wsum, acc, sq_own, sq_other, kv, att, keep, send0, recv0, sends, recvs, fin, pieces,
    sq_ss, sq_rs, kv_ss, kv_rs, a_ss, a_rs, l_ss, l_rs, f_ss, f_rs,
):
    seq = lax.axis_index("seq")
    head = lax.axis_index("head")
    ratio = ns // nh
    levels = int(math.log2(nh))
    chain = ns // 2
    place, side = seq // 2, seq % 2
    core = head % 2
    rows = q_ref.shape[0]
    heads_here = q_ref.shape[1] // HD
    vis = x_ref.shape[0]
    pad = kv.shape[2]
    half = ow_ref.shape[1] // 2
    mate = head + 1 - 2 * core
    across = seq + 1 - 2 * side

    def bit(level):
        return (head // 2**level) % 2

    def partner(level):
        return head + 2**level * (1 - 2 * bit(level))

    chunks = x_ref.shape[1] // CHUNK

    def x_copy(i):
        at = pl.ds(pl.multiple_of(i * CHUNK, CHUNK), CHUNK)
        return pltpu.make_async_copy(x_hbm.at[:, at], x_ref.at[:, at], x_sem.at[i])

    def w_copy(i):
        at = pl.ds(pl.multiple_of(i * CHUNK, CHUNK), CHUNK)
        return pltpu.make_async_copy(w_hbm.at[:, at], w_ref.at[:, at], w_sem.at[i])

    small = [
        pltpu.make_async_copy(source, target, in_sem.at[i])
        for i, (source, target) in enumerate([
            (q_hbm, q_ref), (qg_hbm, qg_ref), (kg_hbm, kg_ref), (cnt_hbm, cnt_ref),
            (span_hbm, span_ref), (ow_hbm, ow_ref),
        ])
    ]
    for i in range(chunks):
        x_copy(i).start()
        w_copy(i).start()
    for copy in small:
        copy.start()

    barrier = pltpu.get_barrier_semaphore()

    def greet(s, h):
        pl.semaphore_signal(barrier, inc=1, device_id=(s, h), device_id_type=MESH)

    def greet_chain(k, carry):
        greet(2 * lax.rem(place + k, chain) + side, head)
        return carry

    lax.fori_loop(1, chain, greet_chain, 0)
    greet(across, head)
    for level in range(levels):
        greet(seq, partner(level))
    for j in range(ratio):
        for h in range(nh):
            source = ratio * head + j

            @pl.when(jnp.logical_or(source != seq, head != h))
            def _():
                greet(source, h)

    acc[...] = jnp.zeros_like(acc)

    def project(i, carry):
        x_copy(i).wait()
        w_copy(i).wait()
        at = pl.ds(pl.multiple_of(i * CHUNK, CHUNK), CHUNK)
        acc[0:vis, :] += dot(x_ref[:, at], w_ref[:, at], NT)
        return carry

    lax.fori_loop(0, chunks, project, 0)
    raw = acc[...]
    lane = lax.broadcasted_iota(jnp.int32, (1, HD), 1)
    low = lane < HD // 2
    squares = jnp.sum(jnp.where(low, raw * raw, 0.0), axis=1, keepdims=True)
    sq_own[...] = jnp.broadcast_to(squares, sq_own.shape)

    expected = (
        chain + levels + ns
        - jnp.where(seq // ratio == head, 1, 0)
    )
    pl.semaphore_wait(barrier, expected)

    sq_copy = pltpu.make_async_remote_copy(
        src_ref=sq_own, dst_ref=sq_other, send_sem=sq_ss, recv_sem=sq_rs,
        device_id=(seq, mate), device_id_type=MESH,
    )
    sq_copy.start()
    for copy in small[:-1]:
        copy.wait()
    left_half, right_half = [], []
    for h in range(heads_here):
        field = q_ref[:, h * HD : (h + 1) * HD].astype(jnp.float32)
        mean_sq = jnp.mean(field * field, axis=1, keepdims=True)
        normed = field / jnp.sqrt(mean_sq + EPSILON) * qg_ref[...]
        normed = normed * (math.log2(math.e) / math.sqrt(HD))
        swapped = pltpu.roll(normed, HD // 2, 1)
        left_half.append(jnp.where(low, 0.0, swapped).astype(jnp.bfloat16))
        right_half.append(jnp.where(low, swapped, 0.0).astype(jnp.bfloat16))
    sq_copy.wait()
    inverse = 1.0 / jnp.sqrt((sq_own[...] + sq_other[...]) / HD + EPSILON)
    gain = kg_ref[...]
    gain = jnp.where(core == 0, gain, pltpu.roll(gain, HD // 2, 1))
    block = jnp.where(low, raw * inverse * gain, raw)
    block = jnp.where(core == 0, pltpu.roll(block, HD // 2, 1), block)
    kv[core, seq] = block.astype(jnp.bfloat16)

    def nearest(i):
        both = jnp.minimum(place, chain - 1 - place)
        t = (i + 1) // 2
        outward = jnp.where(place < chain // 2, -1, 1)
        near = jnp.where(i % 2 == 1, place + outward * t, place - outward * t)
        far = jnp.where(place < chain - 1 - place, place + (i - both), place - (i - both))
        return jnp.where(i <= 2 * both, near, far)

    def kv_copy(s, kind, target):
        return pltpu.make_async_remote_copy(
            src_ref=kv.at[core, s], dst_ref=kv.at[core, s],
            send_sem=kv_ss.at[s, kind], recv_sem=kv_rs.at[core, s],
            device_id=target, device_id_type=MESH,
        )

    def a_copy(s, kind, target):
        return pltpu.make_async_remote_copy(
            src_ref=att.at[s], dst_ref=att.at[s],
            send_sem=a_ss.at[s, kind], recv_sem=a_rs.at[s],
            device_id=target, device_id_type=MESH,
        )

    def spread(copy, act):
        act(copy(seq, chain, (across, head)))

        def one(i, carry):
            at = nearest(i)
            act(copy(seq, at, (2 * at + side, head)))
            return carry

        lax.fori_loop(1, chain, one, 0)

    def start(copy):
        copy.start()

    def wait_send(copy):
        copy.wait_send()

    slots = jnp.concatenate(
        [jnp.concatenate([left, right], axis=1) for left, right in zip(left_half, right_half)], axis=0
    )
    cap = ns * vis // TILES
    span_f = span_ref[...].astype(jnp.float32)
    first = jnp.transpose(jnp.broadcast_to(span_f[0:1, :], (HD, rows)))[:, 0:1]
    end = jnp.transpose(jnp.broadcast_to(span_f[1:2, :], (HD, rows)))[:, 0:1]
    first = jnp.concatenate([first] * heads_here, axis=0)
    end = jnp.concatenate([end] * heads_here, axis=0)
    numer[...] = jnp.zeros_like(numer)
    wsum[...] = jnp.zeros_like(wsum)

    def attend(s):
        pltpu.make_async_remote_copy(
            src_ref=kv.at[1 - core, s], dst_ref=kv.at[1 - core, s],
            send_sem=kv_ss.at[s, chain + 1], recv_sem=kv_rs.at[1 - core, s],
            device_id=(seq, mate), device_id_type=MESH,
        ).wait_recv()
        inside = lax.broadcasted_iota(jnp.int32, (1, pad), 1)
        token = inside + s * vis
        tile = jnp.zeros_like(token)
        count = jnp.full_like(token, cnt_ref[0])
        for t in range(1, TILES):
            tile = jnp.where(token >= t * cap, t, tile)
            count = jnp.where(token >= t * cap, t * cap + cnt_ref[t], count)
        present = jnp.logical_and(inside < vis, token < count)
        tile = jnp.where(present, tile, 2 * TILES).astype(jnp.float32)
        allowed = jnp.logical_and(first <= tile, tile < end)
        both = jnp.concatenate([kv[0, s], kv[1, s]], axis=1)
        weights = jnp.where(allowed, jnp.exp2(dot(slots, both, NT)), 0.0)
        wsum[...] += weights
        numer[...] += dot(weights.astype(jnp.bfloat16), both)

    spread(kv_copy, start)
    kv_copy(seq, chain + 1, (seq, mate)).start()

    def kv_step(i, carry):
        @pl.when(jnp.logical_and(i > 0, i < chain))
        def _():
            s = 2 * nearest(i) + side
            kv_copy(s, chain, (across, head)).wait_recv()
            kv_copy(s, chain, (across, head)).start()
            kv_copy(s, chain + 1, (seq, mate)).start()

        @pl.when(jnp.logical_and(i > 0, i <= chain))
        def _():
            attend(2 * nearest(i - 1) + side)
            s = 2 * nearest(i - 1) + 1 - side
            kv_copy(s, chain + 1, (seq, mate)).wait_recv()
            kv_copy(s, chain + 1, (seq, mate)).start()

        @pl.when(i > 1)
        def _():
            attend(2 * nearest(i - 2) + 1 - side)

        return carry

    lax.fori_loop(1, chain + 2, kv_step, 0)
    for h in range(heads_here):
        at = slice(h * rows, (h + 1) * rows)
        total = jnp.sum(wsum[at], axis=1, keepdims=True)
        mixed = jnp.where(low, numer[at, :HD], numer[at, HD:])
        att[seq, :, h * HD : (h + 1) * HD] = (mixed / total).astype(jnp.bfloat16)
    small[-1].wait()
    spread(a_copy, start)

    def level_refs(level):
        if level == 0:
            return send0, recv0
        return sends[level - 1], recvs[level - 1]

    def level_copy(level, s):
        source, target = level_refs(level)
        return pltpu.make_async_remote_copy(
            src_ref=source.at[s], dst_ref=target.at[s],
            send_sem=l_ss.at[level, s], recv_sem=l_rs.at[level, s],
            device_id=(seq, partner(level)), device_id_type=MESH,
        )

    def final_copy(s):
        return pltpu.make_async_remote_copy(
            src_ref=fin.at[s], dst_ref=pieces.at[seq % ratio, head],
            send_sem=f_ss.at[s], recv_sem=f_rs.at[seq % ratio, head],
            device_id=(s, seq // ratio), device_id_type=MESH,
        )

    def is_mine(s):
        return jnp.logical_and(s == seq, seq // ratio == head)

    def turn(i):
        chained = jnp.where(i == 0, 0, (i + 1) // 2)
        swapped = jnp.where(i == ns - 1, chain - 1, jnp.maximum(i // 2 - 1, 0))
        own_side = jnp.logical_or(i == 0, jnp.logical_and(i % 2 == 1, i < ns - 1))
        at = nearest(jnp.where(own_side, chained, swapped))
        return 2 * at + jnp.where(own_side, side, 1 - side), own_side

    sizes = [rows] + [rows >> level for level in range(1, levels)]

    def kept_at(level):
        off = 0
        for done in range(1, level + 1):
            off = off + bit(done) * sizes[done]
        return off

    def first_stage(i):
        s, own_side = turn(i)

        @pl.when(i > 0)
        def _():
            a_copy(s, chain, (across, head)).wait_recv()

        @pl.when(jnp.logical_and(own_side, i > 0))
        def _():
            a_copy(s, chain, (across, head)).start()

        rows_in = att[s]
        other = pl.ds(pl.multiple_of((1 - core) * half, half), half)
        send0[s] = dot(rows_in, ow_ref[:, other]).astype(jnp.bfloat16)
        level_copy(0, s).start()
        mine = pl.ds(pl.multiple_of(core * half, half), half)
        keep[s] = dot(rows_in, ow_ref[:, mine])

    def later_stage(level, i):
        s, _ = turn(i)
        level_copy(level - 1, s).wait_recv()
        size = sizes[level - 1]
        base = kept_at(level - 1)
        arrived = level_refs(level - 1)[1]
        if level == levels:
            total = keep[s, pl.ds(pl.multiple_of(base, size), size)] + arrived[s].astype(jnp.float32)
            fin[s] = total.astype(jnp.bfloat16)

            @pl.when(is_mine(s))
            def _():
                pieces[seq % ratio, head] = fin[s]

            @pl.when(jnp.logical_not(is_mine(s)))
            def _():
                final_copy(s).start()

        else:
            step = sizes[level]
            out_off = (1 - bit(level)) * step
            in_off = bit(level) * step
            sent = keep[s, pl.ds(pl.multiple_of(base + out_off, step), step)]
            sent = sent + arrived[s, pl.ds(pl.multiple_of(out_off, step), step)].astype(jnp.float32)
            level_refs(level)[0][s] = sent.astype(jnp.bfloat16)
            level_copy(level, s).start()
            at = pl.ds(pl.multiple_of(base + in_off, step), step)
            keep[s, at] = keep[s, at] + arrived[s, pl.ds(pl.multiple_of(in_off, step), step)].astype(jnp.float32)

    def pipeline(i, carry):
        @pl.when(i == 1)
        def _():
            later_stage(1, 0)

        @pl.when(i < ns)
        def _():
            first_stage(i)

        @pl.when(jnp.logical_and(i >= 2, i - 1 < ns))
        def _():
            later_stage(1, i - 1)

        for level in range(2, levels + 1):
            lag = 2 * level - 1

            @pl.when(jnp.logical_and(i >= lag, i - lag < ns))
            def _():
                later_stage(level, i - lag)

        return carry

    lax.fori_loop(0, ns + 2 * levels - 1, pipeline, 0)

    for b in range(ratio):
        for h in range(nh):
            @pl.when(jnp.logical_or(ratio * head + b != seq, head != h))
            def _():
                pltpu.make_async_remote_copy(
                    src_ref=fin.at[0], dst_ref=pieces.at[b, h],
                    send_sem=f_ss.at[0], recv_sem=f_rs.at[b, h],
                    device_id=(across, head), device_id_type=MESH,
                ).wait_recv()

            off = sum(((h >> level) & 1) * sizes[level] for level in range(1, levels))
            col = b * 2 * half + (h & 1) * half
            out_ref[off : off + sizes[-1], col : col + half] = pieces[b, h]

    def finish(s, carry):
        @pl.when(jnp.logical_and(s % 2 == side, s != seq))
        def _():
            kv_copy(s, chain, (across, head)).wait_send()
            a_copy(s, chain, (across, head)).wait_send()

        kv_copy(s, chain + 1, (seq, mate)).wait_send()
        for level in range(levels):
            level_copy(level, s).wait_send()

        @pl.when(jnp.logical_not(is_mine(s)))
        def _():
            final_copy(s).wait_send()

        return carry

    lax.fori_loop(0, ns, finish, 0)
    spread(kv_copy, wait_send)
    spread(a_copy, wait_send)


def local(queries, vision, kv_weight, out_weight, q_gain, k_gain, tile_counts, spans):
    ns, nh = lax.axis_size("seq"), lax.axis_size("head")
    rows, width = queries.shape
    vis, model = vision.shape
    cols = out_weight.shape[1]
    half = cols // 2
    levels = int(math.log2(nh))
    pad = -(-vis // 16) * 16
    weights = jnp.swapaxes(kv_weight, 1, 2).reshape(-1, model)
    bf16, f32 = jnp.bfloat16, jnp.float32
    halved = [pltpu.VMEM((ns, rows >> level, half), bf16) for level in range(1, levels)]
    last = rows >> (levels - 1)
    vmem = pl.BlockSpec(memory_space=pltpu.VMEM)
    dma = pltpu.SemaphoreType.DMA
    return pl.pallas_call(
        functools.partial(kernel, ns, nh),
        out_shape=jax.ShapeDtypeStruct((rows, model // nh), bf16),
        in_specs=[pl.BlockSpec(memory_space=pltpu.HBM)] * 8,
        out_specs=vmem,
        scratch_shapes=[
            pltpu.VMEM((rows, width), bf16),
            pltpu.VMEM((vis, model), bf16),
            pltpu.VMEM((HD, model), bf16),
            pltpu.VMEM((width, cols), bf16),
            pltpu.VMEM((1, HD), f32),
            pltpu.VMEM((1, HD), f32),
            pltpu.SMEM((TILES,), jnp.int32),
            pltpu.VMEM((2, rows), jnp.int32),
            dma((6,)), dma((model // CHUNK,)), dma((model // CHUNK,)),
            pltpu.VMEM((rows * width // HD, 2 * HD), f32),
            pltpu.VMEM((rows * width // HD, pad), f32),
            pltpu.VMEM((pad, HD), f32),
            pltpu.VMEM((pad, HD), f32),
            pltpu.VMEM((pad, HD), f32),
            pltpu.VMEM((2, ns, pad, HD), bf16),
            pltpu.VMEM((ns, rows, width), bf16),
            pltpu.VMEM((ns, rows, half), f32),
            pltpu.VMEM((ns, rows, half), bf16),
            pltpu.VMEM((ns, rows, half), bf16),
            halved,
            list(halved),
            pltpu.VMEM((ns, last, half), bf16),
            pltpu.VMEM((ns // nh, nh, last, half), bf16),
            dma, dma, dma((ns, ns // 2 + 2)), dma((2, ns)), dma((ns, ns // 2 + 1)), dma((ns,)),
            dma((levels, ns)), dma((levels, ns)), dma((ns,)), dma((ns // nh, nh)),
        ],
        compiler_params=pltpu.CompilerParams(
            collective_id=0, has_side_effects=True, vmem_limit_bytes=60 * 2**20
        ),
    )(
        queries, vision, weights, out_weight, q_gain.reshape(1, HD), k_gain.reshape(1, HD),
        tile_counts, jnp.swapaxes(spans, 0, 1),
    )


def solution(mesh):
    return jax.shard_map(
        local,
        mesh=mesh,
        in_specs=(
            P("seq", "head"),
            P("seq", None),
            P(None, None, "head"),
            P("head", "seq"),
            P(),
            P(),
            P(),
            P("seq", None),
        ),
        out_specs=P("seq", "head"),
        check_vma=False,
    )
```

```python
import functools
import math

import jax
import jax.numpy as jnp
from jax import lax
from jax.experimental import pallas as pl
from jax.experimental.pallas import tpu as pltpu
from jax.sharding import PartitionSpec as P

HD = 128
TILES = 4
EPSILON = 1e-05
MESH = pl.DeviceIdType.MESH
NT = (((1,), (1,)), ((), ()))
NN = (((1,), (0,)), ((), ()))
CHUNK = 2048


def dot(x, y, dims=NN):
    return lax.dot_general(x, y, dims, preferred_element_type=jnp.float32)


def kernel(
    ns, nh, q_hbm, x_hbm, w_hbm, ow_hbm, qg_hbm, kg_hbm, cnt_hbm, span_hbm, out_ref,
    q_ref, x_ref, w_ref, ow_ref, qg_ref, kg_ref, cnt_ref, span_ref, in_sem, x_sem, w_sem,
    numer, wsum, acc, sq_own, sq_other, kv, att, keep, send0, recv0, sends, recvs, fin, pieces,
    sq_ss, sq_rs, kv_ss, kv_rs, a_ss, a_rs, l_ss, l_rs, f_ss, f_rs,
):
    seq = lax.axis_index("seq")
    head = lax.axis_index("head")
    ratio = ns // nh
    levels = int(math.log2(nh))
    chain = ns // 2
    place, side = seq // 2, seq % 2
    core = head % 2
    rows = q_ref.shape[0]
    heads_here = q_ref.shape[1] // HD
    vis = x_ref.shape[0]
    pad = kv.shape[2]
    half = ow_ref.shape[1] // 2
    mate = head + 1 - 2 * core
    across = seq + 1 - 2 * side

    def bit(level):
        return (head // 2**level) % 2

    def partner(level):
        return head + 2**level * (1 - 2 * bit(level))

    chunks = x_ref.shape[1] // CHUNK

    def x_copy(i):
        at = pl.ds(pl.multiple_of(i * CHUNK, CHUNK), CHUNK)
        return pltpu.make_async_copy(x_hbm.at[:, at], x_ref.at[:, at], x_sem.at[i])

    def w_copy(i):
        at = pl.ds(pl.multiple_of(i * CHUNK, CHUNK), CHUNK)
        return pltpu.make_async_copy(w_hbm.at[:, at], w_ref.at[:, at], w_sem.at[i])

    small = [
        pltpu.make_async_copy(source, target, in_sem.at[i])
        for i, (source, target) in enumerate([
            (q_hbm, q_ref), (qg_hbm, qg_ref), (kg_hbm, kg_ref), (cnt_hbm, cnt_ref),
            (span_hbm, span_ref), (ow_hbm, ow_ref),
        ])
    ]
    for i in range(chunks):
        x_copy(i).start()
        w_copy(i).start()
    for copy in small:
        copy.start()

    barrier = pltpu.get_barrier_semaphore()

    def greet(s, h):
        pl.semaphore_signal(barrier, inc=1, device_id=(s, h), device_id_type=MESH)

    def greet_chain(k, carry):
        greet(2 * lax.rem(place + k, chain) + side, head)
        return carry

    lax.fori_loop(1, chain, greet_chain, 0)
    greet(across, head)
    for level in range(levels):
        greet(seq, partner(level))
    for j in range(ratio):
        for h in range(nh):
            source = ratio * head + j

            @pl.when(jnp.logical_or(source != seq, head != h))
            def _():
                greet(source, h)

    acc[...] = jnp.zeros_like(acc)

    def project(i, carry):
        x_copy(i).wait()
        w_copy(i).wait()
        at = pl.ds(pl.multiple_of(i * CHUNK, CHUNK), CHUNK)
        acc[0:vis, :] += dot(x_ref[:, at], w_ref[:, at], NT)
        return carry

    lax.fori_loop(0, chunks, project, 0)
    raw = acc[...]
    lane = lax.broadcasted_iota(jnp.int32, (1, HD), 1)
    low = lane < HD // 2
    squares = jnp.sum(jnp.where(low, raw * raw, 0.0), axis=1, keepdims=True)
    sq_own[...] = jnp.broadcast_to(squares, sq_own.shape)

    expected = (
        chain + levels + ns
        - jnp.where(seq // ratio == head, 1, 0)
    )
    pl.semaphore_wait(barrier, expected)

    sq_copy = pltpu.make_async_remote_copy(
        src_ref=sq_own, dst_ref=sq_other, send_sem=sq_ss, recv_sem=sq_rs,
        device_id=(seq, mate), device_id_type=MESH,
    )
    sq_copy.start()
    for copy in small[:-1]:
        copy.wait()
    left_half, right_half = [], []
    for h in range(heads_here):
        field = q_ref[:, h * HD : (h + 1) * HD].astype(jnp.float32)
        mean_sq = jnp.mean(field * field, axis=1, keepdims=True)
        normed = field / jnp.sqrt(mean_sq + EPSILON) * qg_ref[...]
        swapped = pltpu.roll(normed, HD // 2, 1)
        left_half.append(jnp.where(low, 0.0, swapped).astype(jnp.bfloat16))
        right_half.append(jnp.where(low, swapped, 0.0).astype(jnp.bfloat16))
    sq_copy.wait()
    inverse = 1.0 / jnp.sqrt((sq_own[...] + sq_other[...]) / HD + EPSILON)
    gain = kg_ref[...]
    gain = jnp.where(core == 0, gain, pltpu.roll(gain, HD // 2, 1))
    block = jnp.where(low, raw * inverse * gain, raw)
    block = jnp.where(core == 0, pltpu.roll(block, HD // 2, 1), block)
    kv[core, seq] = block.astype(jnp.bfloat16)

    def nearest(i):
        both = jnp.minimum(place, chain - 1 - place)
        t = (i + 1) // 2
        near = jnp.where(i % 2 == 1, place - t, place + t)
        far = jnp.where(place < chain - 1 - place, place + (i - both), place - (i - both))
        return jnp.where(i <= 2 * both, near, far)

    def kv_copy(s, kind, target):
        return pltpu.make_async_remote_copy(
            src_ref=kv.at[core, s], dst_ref=kv.at[core, s],
            send_sem=kv_ss.at[s, kind], recv_sem=kv_rs.at[core, s],
            device_id=target, device_id_type=MESH,
        )

    def a_copy(s, kind, target):
        return pltpu.make_async_remote_copy(
            src_ref=att.at[s], dst_ref=att.at[s],
            send_sem=a_ss.at[s, kind], recv_sem=a_rs.at[s],
            device_id=target, device_id_type=MESH,
        )

    def spread(copy, act):
        act(copy(seq, chain, (across, head)))

        def one(i, carry):
            at = nearest(i)
            act(copy(seq, at, (2 * at + side, head)))
            return carry

        lax.fori_loop(1, chain, one, 0)

    def start(copy):
        copy.start()

    def wait_send(copy):
        copy.wait_send()

    slots = jnp.concatenate(
        [jnp.concatenate([left, right], axis=1) for left, right in zip(left_half, right_half)], axis=0
    )
    cap = ns * vis // TILES
    span_f = span_ref[...].astype(jnp.float32)
    first = jnp.transpose(jnp.broadcast_to(span_f[0:1, :], (HD, rows)))[:, 0:1]
    end = jnp.transpose(jnp.broadcast_to(span_f[1:2, :], (HD, rows)))[:, 0:1]
    first = jnp.concatenate([first] * heads_here, axis=0)
    end = jnp.concatenate([end] * heads_here, axis=0)
    scale = math.log2(math.e) / math.sqrt(HD)
    numer[...] = jnp.zeros_like(numer)
    wsum[...] = jnp.zeros_like(wsum)

    def attend(s):
        pltpu.make_async_remote_copy(
            src_ref=kv.at[1 - core, s], dst_ref=kv.at[1 - core, s],
            send_sem=kv_ss.at[s, chain + 1], recv_sem=kv_rs.at[1 - core, s],
            device_id=(seq, mate), device_id_type=MESH,
        ).wait_recv()
        inside = lax.broadcasted_iota(jnp.int32, (1, pad), 1)
        token = inside + s * vis
        tile = jnp.zeros_like(token)
        count = jnp.full_like(token, cnt_ref[0])
        for t in range(1, TILES):
            tile = jnp.where(token >= t * cap, t, tile)
            count = jnp.where(token >= t * cap, t * cap + cnt_ref[t], count)
        present = jnp.logical_and(inside < vis, token < count)
        tile = jnp.where(present, tile, 2 * TILES).astype(jnp.float32)
        allowed = jnp.logical_and(first <= tile, tile < end)
        both = jnp.concatenate([kv[0, s], kv[1, s]], axis=1)
        weights = jnp.where(allowed, jnp.exp2(dot(slots, both, NT) * scale), 0.0)
        wsum[...] += weights
        numer[...] += dot(weights.astype(jnp.bfloat16), both)

    spread(kv_copy, start)
    kv_copy(seq, chain + 1, (seq, mate)).start()

    def kv_step(i, carry):
        @pl.when(jnp.logical_and(i > 0, i < chain))
        def _():
            s = 2 * nearest(i) + side
            kv_copy(s, chain, (across, head)).wait_recv()
            kv_copy(s, chain, (across, head)).start()
            kv_copy(s, chain + 1, (seq, mate)).start()

        @pl.when(jnp.logical_and(i > 0, i <= chain))
        def _():
            attend(2 * nearest(i - 1) + side)
            s = 2 * nearest(i - 1) + 1 - side
            kv_copy(s, chain + 1, (seq, mate)).wait_recv()
            kv_copy(s, chain + 1, (seq, mate)).start()

        @pl.when(i > 1)
        def _():
            attend(2 * nearest(i - 2) + 1 - side)

        return carry

    lax.fori_loop(1, chain + 2, kv_step, 0)
    for h in range(heads_here):
        at = slice(h * rows, (h + 1) * rows)
        total = jnp.sum(wsum[at], axis=1, keepdims=True)
        mixed = jnp.where(low, numer[at, :HD], numer[at, HD:])
        att[seq, :, h * HD : (h + 1) * HD] = (mixed / total).astype(jnp.bfloat16)
    small[-1].wait()
    spread(a_copy, start)

    def level_refs(level):
        if level == 0:
            return send0, recv0
        return sends[level - 1], recvs[level - 1]

    def level_copy(level, s):
        source, target = level_refs(level)
        return pltpu.make_async_remote_copy(
            src_ref=source.at[s], dst_ref=target.at[s],
            send_sem=l_ss.at[level, s], recv_sem=l_rs.at[level, s],
            device_id=(seq, partner(level)), device_id_type=MESH,
        )

    def final_copy(s):
        return pltpu.make_async_remote_copy(
            src_ref=fin.at[s], dst_ref=pieces.at[seq % ratio, head],
            send_sem=f_ss.at[s], recv_sem=f_rs.at[seq % ratio, head],
            device_id=(s, seq // ratio), device_id_type=MESH,
        )

    def is_mine(s):
        return jnp.logical_and(s == seq, seq // ratio == head)

    def turn(i):
        chained = jnp.where(i == 0, 0, (i + 1) // 2)
        swapped = jnp.where(i == ns - 1, chain - 1, jnp.maximum(i // 2 - 1, 0))
        own_side = jnp.logical_or(i == 0, jnp.logical_and(i % 2 == 1, i < ns - 1))
        at = nearest(jnp.where(own_side, chained, swapped))
        return 2 * at + jnp.where(own_side, side, 1 - side), own_side

    sizes = [rows] + [rows >> level for level in range(1, levels)]

    def kept_at(level):
        off = 0
        for done in range(1, level + 1):
            off = off + bit(done) * sizes[done]
        return off

    def first_stage(i):
        s, own_side = turn(i)

        @pl.when(jnp.logical_not(own_side))
        def _():
            a_copy(s, chain, (across, head)).wait_recv()

        rows_in = att[s]
        other = pl.ds(pl.multiple_of((1 - core) * half, half), half)
        send0[s] = dot(rows_in, ow_ref[:, other]).astype(jnp.bfloat16)
        level_copy(0, s).start()
        mine = pl.ds(pl.multiple_of(core * half, half), half)
        keep[s] = dot(rows_in, ow_ref[:, mine])

    def forward(k):
        s = 2 * nearest(k) + side
        a_copy(s, chain, (across, head)).wait_recv()
        a_copy(s, chain, (across, head)).start()

    def later_stage(level, i):
        s, _ = turn(i)
        level_copy(level - 1, s).wait_recv()
        size = sizes[level - 1]
        base = kept_at(level - 1)
        arrived = level_refs(level - 1)[1]
        if level == levels:
            total = keep[s, pl.ds(pl.multiple_of(base, size), size)] + arrived[s].astype(jnp.float32)
            fin[s] = total.astype(jnp.bfloat16)

            @pl.when(is_mine(s))
            def _():
                pieces[seq % ratio, head] = fin[s]

            @pl.when(jnp.logical_not(is_mine(s)))
            def _():
                final_copy(s).start()

        else:
            step = sizes[level]
            out_off = (1 - bit(level)) * step
            in_off = bit(level) * step
            sent = keep[s, pl.ds(pl.multiple_of(base + out_off, step), step)]
            sent = sent + arrived[s, pl.ds(pl.multiple_of(out_off, step), step)].astype(jnp.float32)
            level_refs(level)[0][s] = sent.astype(jnp.bfloat16)
            level_copy(level, s).start()
            at = pl.ds(pl.multiple_of(base + in_off, step), step)
            keep[s, at] = keep[s, at] + arrived[s, pl.ds(pl.multiple_of(in_off, step), step)].astype(jnp.float32)

    def pipeline(i, carry):
        @pl.when(i == 1)
        def _():
            later_stage(1, 0)
            forward(1)

        @pl.when(i < ns)
        def _():
            first_stage(i)

        @pl.when(jnp.logical_and(i % 2 == 0, jnp.logical_and(i >= 2, i < ns - 2)))
        def _():
            forward(i // 2 + 1)

        @pl.when(jnp.logical_and(i >= 2, i - 1 < ns))
        def _():
            later_stage(1, i - 1)

        for level in range(2, levels + 1):
            lag = 2 * level - 1

            @pl.when(jnp.logical_and(i >= lag, i - lag < ns))
            def _():
                later_stage(level, i - lag)

        return carry

    lax.fori_loop(0, ns + 2 * levels - 1, pipeline, 0)

    for b in range(ratio):
        for h in range(nh):
            @pl.when(jnp.logical_or(ratio * head + b != seq, head != h))
            def _():
                pltpu.make_async_remote_copy(
                    src_ref=fin.at[0], dst_ref=pieces.at[b, h],
                    send_sem=f_ss.at[0], recv_sem=f_rs.at[b, h],
                    device_id=(across, head), device_id_type=MESH,
                ).wait_recv()

            off = sum(((h >> level) & 1) * sizes[level] for level in range(1, levels))
            col = b * 2 * half + (h & 1) * half
            out_ref[off : off + sizes[-1], col : col + half] = pieces[b, h]

    def finish(s, carry):
        @pl.when(jnp.logical_and(s % 2 == side, s != seq))
        def _():
            kv_copy(s, chain, (across, head)).wait_send()
            a_copy(s, chain, (across, head)).wait_send()

        kv_copy(s, chain + 1, (seq, mate)).wait_send()
        for level in range(levels):
            level_copy(level, s).wait_send()

        @pl.when(jnp.logical_not(is_mine(s)))
        def _():
            final_copy(s).wait_send()

        return carry

    lax.fori_loop(0, ns, finish, 0)
    spread(kv_copy, wait_send)
    spread(a_copy, wait_send)


def local(queries, vision, kv_weight, out_weight, q_gain, k_gain, tile_counts, spans):
    ns, nh = lax.axis_size("seq"), lax.axis_size("head")
    rows, width = queries.shape
    vis, model = vision.shape
    cols = out_weight.shape[1]
    half = cols // 2
    levels = int(math.log2(nh))
    pad = -(-vis // 16) * 16
    weights = jnp.swapaxes(kv_weight, 1, 2).reshape(-1, model)
    bf16, f32 = jnp.bfloat16, jnp.float32
    halved = [pltpu.VMEM((ns, rows >> level, half), bf16) for level in range(1, levels)]
    last = rows >> (levels - 1)
    vmem = pl.BlockSpec(memory_space=pltpu.VMEM)
    dma = pltpu.SemaphoreType.DMA
    return pl.pallas_call(
        functools.partial(kernel, ns, nh),
        out_shape=jax.ShapeDtypeStruct((rows, model // nh), bf16),
        in_specs=[pl.BlockSpec(memory_space=pltpu.HBM)] * 8,
        out_specs=vmem,
        scratch_shapes=[
            pltpu.VMEM((rows, width), bf16),
            pltpu.VMEM((vis, model), bf16),
            pltpu.VMEM((HD, model), bf16),
            pltpu.VMEM((width, cols), bf16),
            pltpu.VMEM((1, HD), f32),
            pltpu.VMEM((1, HD), f32),
            pltpu.SMEM((TILES,), jnp.int32),
            pltpu.VMEM((2, rows), jnp.int32),
            dma((6,)), dma((model // CHUNK,)), dma((model // CHUNK,)),
            pltpu.VMEM((rows * width // HD, 2 * HD), f32),
            pltpu.VMEM((rows * width // HD, pad), f32),
            pltpu.VMEM((pad, HD), f32),
            pltpu.VMEM((pad, HD), f32),
            pltpu.VMEM((pad, HD), f32),
            pltpu.VMEM((2, ns, pad, HD), bf16),
            pltpu.VMEM((ns, rows, width), bf16),
            pltpu.VMEM((ns, rows, half), f32),
            pltpu.VMEM((ns, rows, half), bf16),
            pltpu.VMEM((ns, rows, half), bf16),
            halved,
            list(halved),
            pltpu.VMEM((ns, last, half), bf16),
            pltpu.VMEM((ns // nh, nh, last, half), bf16),
            dma, dma, dma((ns, ns // 2 + 2)), dma((2, ns)), dma((ns, ns // 2 + 1)), dma((ns,)),
            dma((levels, ns)), dma((levels, ns)), dma((ns,)), dma((ns // nh, nh)),
        ],
        compiler_params=pltpu.CompilerParams(
            collective_id=0, has_side_effects=True, vmem_limit_bytes=60 * 2**20
        ),
    )(
        queries, vision, weights, out_weight, q_gain.reshape(1, HD), k_gain.reshape(1, HD),
        tile_counts, jnp.swapaxes(spans, 0, 1),
    )


def solution(mesh):
    return jax.shard_map(
        local,
        mesh=mesh,
        in_specs=(
            P("seq", "head"),
            P("seq", None),
            P(None, None, "head"),
            P("head", "seq"),
            P(),
            P(),
            P(),
            P("seq", None),
        ),
        out_specs=P("seq", "head"),
        check_vma=False,
    )
```
